32 devices in a mesh: row: 4 (over z), col: 8 (over y, x, core).
Axes of the slice: x: 2, y: 2, z: 4, core: 2. Of those that a mesh axis runs over, the one named last changes fastest.
Arguments:
- new_keys: bfloat16 [256, 28672], P('col', 'row'), may hold values from -6 to 6
- precision: bfloat16 [28672, 28672], P('row', 'col'), may hold values from -0.03125 to 0.03125
- stored_keys: bfloat16 [8, 256, 28672], P('row', None, 'col'), may hold values from -0.03125 to 0.03125
- pair_batch: int32 [4, 6], replicated, may hold values from 0 to 7, as said below
- pair_count: int32 [4], replicated, may hold values from 2 to 6, as said below
- batch_length: int32 [8], replicated, may hold values from 64 to 256
- batch_slot: int32 [8], replicated, may hold values from 0 to 7, each once
Outputs:
- whitened: bfloat16 [256, 28672], P('row', 'col')
- intersections: float32 [4, 6, 64, 256], P('row', None, 'col')
The draws below stay inside these ranges and needn't reach their ends.
Inputs may be any that keep to these rules, and one draw needn't show every extreme that they name: `pair_batch`: the ids in one block's row are distinct; ids at places at or beyond the block's count are ignored. `pair_count`: some block lists exactly 6 batches. `batch_slot`: every store slot belongs to exactly one batch.
All inputs are finite; a program needn't handle non-finite values.
Results may differ from the reference program's by a relative error of at most 0.0029.
Values may be sent and summed in bfloat16 or wider, within the bound.
No kernel may reach another device: no remote copies, remote signals or barrier semaphores. Data moves between devices by JAX's collectives and lax.ppermute only.
A program may use at most 128 MiB of HBM per device.

```python
import jax
import jax.numpy as jnp
from jax import lax

ORDER = 28672
KB = 64
BK = 256
NBLK = 4
NK = 256
NB = 8
MAXP = 6
MINP = 2


def draw_pair_batch(key, part):
    scores = jax.random.randint(key, (NBLK, NB), 0, 1 << 20) * NB + jnp.arange(NB, dtype=jnp.int32)[None, :]
    order = jnp.argsort(scores, axis=1, stable=True)
    return order[:, :MAXP].astype(jnp.int32)


def draw_pair_count(key, part):
    counts = jax.random.randint(key, (NBLK,), MINP, MAXP + 1)
    chosen = jax.random.randint(jax.random.fold_in(key, 7), (), 0, NBLK)
    return counts.at[chosen].set(MAXP).astype(jnp.int32)


def with_ends(entries, key, low, top_value):
    shape = entries.shape
    index_at = [jax.random.randint(jax.random.fold_in(key, axis), (), 0, shape[axis]) for axis in range(len(shape))]
    entries = entries.at[tuple(index_at)].set(low)
    longest = shape.index(max(shape))
    index_at[longest] = (index_at[longest] + 1) % shape[longest]
    return entries.at[tuple(index_at)].set(top_value)


def strengthened(entries, stream_key, source, target, blocks, factor):
    owner, partner = [(jnp.arange(entries.shape[axis_at]) // (entries.shape[axis_at] // blocks)).reshape([-1 if axis == axis_at else 1 for axis in range(entries.ndim)]) for axis_at in (source, target)]
    chosen = jax.random.permutation(stream_key, blocks)[partner]
    strong = (owner == chosen) | (owner == (partner + blocks // 2) % blocks)
    return jnp.where(strong, factor * entries, entries)


def steps_of(stream_key, shape, split, smallest, largest):
    def one(position, blocks):
        heights = jax.random.uniform(jax.random.fold_in(jax.random.fold_in(stream_key, 6), position), (blocks,), jnp.float32, smallest / len(split), largest / len(split))
        return jnp.repeat(jnp.exp(heights), shape[position] // blocks).reshape((-1,) + (1,) * (len(shape) - position - 1))

    level = one(*split[0])
    for cut in split[1:]:
        level = level * one(*cut)
    return level


def normal_values(stream_key, dims, scale, limit, cuts=(), held_as=jnp.bfloat16):
    drawn = jax.random.normal(stream_key, dims, jnp.float32) * scale
    if len(cuts) > 0:
        drawn = steps_of(stream_key, dims, cuts, -0.22, 0.18) * drawn
    return jnp.clip(drawn, min=-limit, max=limit).astype(held_as)


def noise_with(own_key, shape, deviation, bound, cuts, heavy, held_as=jnp.bfloat16):
    array = deviation * jax.random.normal(own_key, shape, jnp.float32)
    if cuts:
        array = array * steps_of(own_key, shape, cuts, -0.22, 0.18)
    return jnp.clip(strengthened(array, jax.random.fold_in(own_key, 3), *heavy), -bound, bound).astype(held_as)


def setup_inputs(seed: int = 0) -> dict:
    seeds = jax.random.split(jax.random.key(seed), 8)
    return {
        "new_keys": noise_with(seeds[0], (NK, ORDER), 1.0, 6.0, ((0, 8), (1, 4)), (1, 0, 8, 2.0)),
        "precision": normal_values(seeds[1], (ORDER, ORDER), ORDER ** -0.5, 0.03125, ((0, 4), (1, 8))),
        "stored_keys": normal_values(seeds[2], (NB, BK, ORDER), ORDER ** -0.5, 0.03125, ((0, 4), (2, 8))),
        "pair_batch": draw_pair_batch(jax.random.fold_in(seeds[7], 71), 0),
        "pair_count": draw_pair_count(jax.random.fold_in(seeds[7], 71), 0),
        "batch_length": with_ends(jax.random.randint(seeds[5], (NB,), BK // 4, BK + 1), jax.random.fold_in(seeds[5], 1), BK // 4, BK).astype(jnp.int32),
        "batch_slot": jax.random.permutation(seeds[6], NB).astype(jnp.int32),
    }


def reference(new_keys, precision, stored_keys, pair_batch, pair_count, batch_length, batch_slot):
    whitened = jnp.dot(new_keys, precision, preferred_element_type=jnp.float32).astype(jnp.bfloat16)
    key_slots = jnp.arange(BK, dtype=jnp.int32)

    def one_block(block):
        rows = lax.dynamic_slice_in_dim(whitened, (block * KB).astype(jnp.int32), KB, 0)

        def one_pair(place):
            batch = pair_batch[block, place]
            slot = batch_slot[batch]
            stored = lax.dynamic_index_in_dim(stored_keys, slot, 0, keepdims=False)
            raw = jnp.dot(rows, stored.T, preferred_element_type=jnp.float32)
            keep = (place < pair_count[block]) & (key_slots < batch_length[batch])
            return jnp.where(keep[None, :], raw, jnp.zeros_like(raw))

        return lax.map(one_pair, jnp.arange(MAXP, dtype=jnp.int32))

    intersections = lax.map(one_block, jnp.arange(NBLK, dtype=jnp.int32))
    return whitened, intersections
```

```python
import functools

import jax
import jax.numpy as jnp
from jax import lax
from jax.experimental import pallas as pl
from jax.experimental.pallas import tpu as pltpu
from jax.sharding import PartitionSpec as P

PARTS = 7
STEPS = 7


def flipped(array, bit, count):
    return lax.ppermute(array, "col", [(c, c ^ bit) for c in range(count)])


def gathered(new_keys, col_count, col_index):
    rows = new_keys.shape[0]
    if col_count != 8:
        return [lax.all_gather(new_keys, "col", axis=0, tiled=True)], [jnp.int32(0)]
    half = rows // 2
    by_x = flipped(new_keys, 2, 8)
    by_y = flipped(new_keys, 4, 8)
    by_core = flipped(new_keys, 1, 8)
    low = flipped(by_x[:half], 4, 8)
    high = flipped(by_y[half:], 2, 8)
    x_core = flipped(by_x, 1, 8)
    y_core = flipped(by_y, 1, 8)
    low_core = flipped(low, 1, 8)
    high_core = flipped(high, 1, 8)
    pieces = [new_keys, by_core, by_x, x_core, by_y, y_core, low, high, low_core, high_core]
    of = [0, 1, 2, 3, 4, 5, 6, 6, 7, 7]
    within = [0] * 7 + [half, 0, half]
    return pieces, [(col_index ^ f) * rows + w for f, w in zip(of, within)]


def product_kernel(count, starts_ref, *refs):
    pieces, weights_ref, wide_ref, sent_ref, keys_ref = refs[:count], *refs[count:]
    step = pl.program_id(0)
    for i, piece in enumerate(pieces):
        size = piece.shape[0]
        keys_ref[pl.ds(pl.multiple_of(starts_ref[i], 16), size), :] = piece[...]
    part = jnp.dot(keys_ref[...], weights_ref[...], preferred_element_type=jnp.float32)

    @pl.when(step == 0)
    def _():
        wide_ref[...] = part

    @pl.when(step > 0)
    def _():
        wide_ref[...] += part

    @pl.when(step == pl.num_programs(0) - 1)
    def _():
        sent_ref[...] = wide_ref[...].astype(sent_ref.dtype)


def product(pieces, starts, weights, part, keys, wire):
    depth, columns = weights.shape
    deep, wide = depth // STEPS, columns // PARTS
    grid_spec = pltpu.PrefetchScalarGridSpec(
        num_scalar_prefetch=1,
        grid=(STEPS,),
        in_specs=[pl.BlockSpec((p.shape[0], deep), lambda k, s: (0, k)) for p in pieces]
        + [pl.BlockSpec((deep, wide), lambda k, s: (k, part))],
        out_specs=[pl.BlockSpec((keys, wide), lambda k, s: (0, 0))] * 2,
        scratch_shapes=[pltpu.VMEM((keys, deep), pieces[0].dtype)],
    )
    return pl.pallas_call(
        functools.partial(product_kernel, len(pieces)),
        grid_spec=grid_spec,
        out_shape=[
            jax.ShapeDtypeStruct((keys, wide), jnp.float32),
            jax.ShapeDtypeStruct((keys, wide), wire),
        ],
        compiler_params=pltpu.CompilerParams(vmem_limit_bytes=24 * 2**20),
        cost_estimate=pl.CostEstimate(
            flops=2 * keys * depth * wide,
            bytes_accessed=2 * depth * (keys + wide) + 6 * keys * wide,
            transcendentals=0,
        ),
        name="product",
    )(starts, *pieces, weights)


def summed(wide, sent, row_count, wire, inner):
    half = row_count // 2
    total = wide
    for hop in range(half - 1):
        came = lax.ppermute(sent, "row", [(hop, hop + 1), (row_count - 1 - hop, row_count - 2 - hop)])
        total = total + came.astype(jnp.float32)
        sent = total.astype(wire)
    came = lax.ppermute(sent, "row", [(half - 1, half), (half, half - 1)])
    final = (total + came.astype(jnp.float32)).astype(jnp.bfloat16)
    for hop in range(half - 1):
        low, high = half - 1 - hop, half + hop
        came = lax.ppermute(final, "row", [(low, low - 1), (high, high + 1)])
        last = hop == half - 2
        if last:
            return final, came
        final = jnp.where(inner[hop], final, came)
    return final, final


def contract_kernel(first, at_ref, final_ref, came_ref, stored_ref, *refs):
    terms_ref, whitened_ref, rows_ref = refs[-3:]
    own, start = at_ref[0], at_ref[1]

    @pl.when(own != 0)
    def _():
        rows_ref[...] = final_ref[...]

    @pl.when(own == 0)
    def _():
        rows_ref[...] = came_ref[...]

    batches, slots, wide = stored_ref.shape
    term = lax.dot_general(
        rows_ref[...],
        stored_ref[...].reshape(batches * slots, wide),
        (((1,), (1,)), ((), ())),
        preferred_element_type=jnp.float32,
    )
    terms_ref[...] = term if first else refs[0][...] + term
    whitened_ref[...] = rows_ref[pl.ds(pl.multiple_of(start, 16), whitened_ref.shape[0]), :]


def contract(at, final, came, stored, terms, whitened, part, block):
    keys, wide = final.shape
    batches, slots, columns = stored.shape
    first = terms is None
    whole = pl.BlockSpec((keys, wide), lambda i, s: (0, 0))
    sums = pl.BlockSpec((keys, batches * slots), lambda i, s: (0, 0))
    in_specs = [whole, whole, pl.BlockSpec((batches, slots, wide), lambda i, s: (0, 0, part))]
    operands = [at, final, came, stored]
    aliases = {}
    if not first:
        in_specs += [sums, pl.BlockSpec(memory_space=pl.ANY)]
        operands += [terms, whitened]
        aliases = {4: 0, 5: 1}
    return pl.pallas_call(
        functools.partial(contract_kernel, first),
        grid_spec=pltpu.PrefetchScalarGridSpec(
            num_scalar_prefetch=1,
            grid=(1,),
            in_specs=in_specs,
            out_specs=[sums, pl.BlockSpec((block, wide), lambda i, s: (0, part))],
            scratch_shapes=[pltpu.VMEM((keys, wide), jnp.bfloat16)],
        ),
        out_shape=[
            jax.ShapeDtypeStruct((keys, batches * slots), jnp.float32),
            jax.ShapeDtypeStruct((block, columns), jnp.bfloat16),
        ],
        input_output_aliases=aliases,
        compiler_params=pltpu.CompilerParams(vmem_limit_bytes=24 * 2**20),
        cost_estimate=pl.CostEstimate(
            flops=2 * keys * wide * batches * slots,
            bytes_accessed=2 * wide * (2 * keys + batches * slots) + 8 * keys * batches * slots,
            transcendentals=0,
        ),
        name="contract",
    )(*operands)


def select_kernel(count, row_ref, batch_ref, used_ref, length_ref, slot_ref, *refs):
    parts, out_ref, held_ref = refs[:count], refs[count], refs[count + 1]
    batches, rows, slots = held_ref.shape[1:]
    for i, part in enumerate(parts):
        for b in range(batches):
            held_ref[i, b] = part[0, :, b * slots : (b + 1) * slots]
    row = row_ref[0]
    column = lax.broadcasted_iota(jnp.int32, (rows, slots), 1)
    for place in range(out_ref.shape[1]):
        batch = batch_ref[row, place]
        slot = slot_ref[batch]
        owner = lax.div(slot, batches)
        shift = lax.rem(row - owner + count, count)
        length = jnp.where(place < used_ref[row], length_ref[batch], 0)
        value = held_ref[shift, slot - owner * batches]
        out_ref[0, place] = jnp.where(column < length, value, 0.0)


def selected(parts, row_index, pair_batch, pair_count, batch_length, batch_slot, batches):
    count = len(parts)
    _, rows, wide = parts[0].shape
    slots = wide // batches
    places = pair_batch.shape[1]
    return pl.pallas_call(
        functools.partial(select_kernel, count),
        grid_spec=pltpu.PrefetchScalarGridSpec(
            num_scalar_prefetch=5,
            grid=(1,),
            in_specs=[pl.BlockSpec((1, rows, wide), lambda i, *s: (0, 0, 0))] * count,
            out_specs=pl.BlockSpec((1, places, rows, slots), lambda i, *s: (0, 0, 0, 0)),
            scratch_shapes=[pltpu.VMEM((count, batches, rows, slots), jnp.float32)],
        ),
        out_shape=jax.ShapeDtypeStruct((1, places, rows, slots), jnp.float32),
        name="select",
    )(row_index[None], pair_batch, pair_count, batch_length, batch_slot, *parts)


def shards(new_keys, precision, stored_keys, pair_batch, pair_count, batch_length, batch_slot):
    row_count = lax.axis_size("row")
    col_count = lax.axis_size("col")
    row_index = lax.axis_index("row")
    col_index = lax.axis_index("col")
    keys = new_keys.shape[0] * col_count
    block = keys // row_count
    batches = stored_keys.shape[0]
    half = row_count // 2
    wire = jnp.bfloat16 if row_count <= 4 else jnp.float32

    away = jnp.where(row_index < half, half - 1 - row_index, row_index - half)
    inner = [away <= hop for hop in range(half)]
    at = jnp.stack([(away < half - 1).astype(jnp.int32), row_index * block])

    pieces, starts = gathered(new_keys, col_count, col_index)
    starts = jnp.stack(starts)
    terms = whitened = None
    for part in range(PARTS):
        wide, sent = product(pieces, starts, precision, part, keys, wire)
        final, came = summed(wide, sent, row_count, wire, inner)
        terms, whitened = contract(at, final, came, stored_keys, terms, whitened, part, block)

    share = block // col_count
    sums = terms.reshape(row_count, col_count, share, terms.shape[1])
    bit = 1
    while bit < col_count:
        pairs = sums.reshape(row_count, sums.shape[1] // 2, 2, share, sums.shape[3])
        mine = (col_index // bit) % 2
        kept = lax.dynamic_index_in_dim(pairs, mine, 2, keepdims=False)
        left = lax.dynamic_index_in_dim(pairs, 1 - mine, 2, keepdims=False)
        sums = kept + flipped(left, bit, col_count)
        bit *= 2
    sums = sums[:, 0]
    parts = []
    for shift in range(row_count):
        part = lax.dynamic_slice_in_dim(sums, (row_index + shift) % row_count, 1, 0)
        if shift:
            part = lax.ppermute(part, "row", [(r, (r + shift) % row_count) for r in range(row_count)])
        parts.append(part)
    shares = selected(parts, row_index, pair_batch, pair_count, batch_length, batch_slot, batches)
    return (whitened, shares)


def solution(mesh):
    placed = (P("col", "row"), P("row", "col"), P("row", None, "col"), P(), P(), P(), P())
    return jax.shard_map(
        shards,
        mesh=mesh,
        in_specs=placed,
        out_specs=(P("row", "col"), P("row", None, "col", None)),
        check_vma=False,
    )
```

```python
import functools

import jax
import jax.numpy as jnp
from jax import lax
from jax.experimental import pallas as pl
from jax.experimental.pallas import tpu as pltpu
from jax.sharding import PartitionSpec as P

PARTS = 5
STEPS = 7
SLOTS = 4
LANES = 128
VMEM = pl.BlockSpec(memory_space=pltpu.VMEM)
ANY = pl.BlockSpec(memory_space=pl.ANY)
SMEM = pl.BlockSpec(memory_space=pltpu.SMEM)


def flipped(array, bit, count):
    return lax.ppermute(array, "col", [(c, c ^ bit) for c in range(count)])


def gathered(new_keys, col_count, col_index):
    rows = new_keys.shape[0]
    if col_count != 8:
        return [lax.all_gather(new_keys, "col", axis=0, tiled=True)], [jnp.int32(0)]
    half = rows // 2
    by_x = flipped(new_keys, 2, 8)
    by_y = flipped(new_keys, 4, 8)
    by_core = flipped(new_keys, 1, 8)
    low = flipped(by_x[:half], 4, 8)
    high = flipped(by_y[half:], 2, 8)
    x_core = flipped(by_x, 1, 8)
    y_core = flipped(by_y, 1, 8)
    low_core = flipped(low, 1, 8)
    high_core = flipped(high, 1, 8)
    pieces = [new_keys, by_core, by_x, x_core, by_y, y_core, low, high, low_core, high_core]
    of = [0, 1, 2, 3, 4, 5, 6, 6, 7, 7]
    within = [0] * 7 + [half, 0, half]
    return pieces, [(col_index ^ f) * rows + w for f, w in zip(of, within)]


def ranges(columns):
    tiles = columns // LANES
    count = min(PARTS, tiles)
    ends = [(tiles * (i + 1) + count // 2) // count * LANES for i in range(count)]
    return list(zip([0] + ends[:-1], ends))


def params():
    return pltpu.CompilerParams(vmem_limit_bytes=32 * 2**20)


def assemble_kernel(count, starts_ref, *refs):
    keys_ref = refs[count]
    for i, piece in enumerate(refs[:count]):
        keys_ref[pl.ds(pl.multiple_of(starts_ref[i], 16), piece.shape[0]), :] = piece[...]


def assembled(pieces, starts, keys):
    return pl.pallas_call(
        functools.partial(assemble_kernel, len(pieces)),
        in_specs=[SMEM] + [VMEM] * len(pieces),
        out_specs=VMEM,
        out_shape=jax.ShapeDtypeStruct((keys, pieces[0].shape[1]), pieces[0].dtype),
        compiler_params=params(),
        name="assemble",
    )(starts, *pieces)


def product_kernel(left, keys_ref, weights_ref, after_ref, wide_ref, sent_ref, held_ref, arrived):
    wide = wide_ref.shape[1]
    deep = held_ref.shape[1]

    def copy(step):
        return pltpu.make_async_copy(
            weights_ref.at[pl.ds(step * deep, deep), pl.ds(left, wide)],
            held_ref.at[step % SLOTS],
            arrived.at[step % SLOTS],
        )

    for step in range(min(SLOTS, STEPS)):
        copy(step).start()
    for step in range(STEPS):
        copy(step).wait()
        part = jnp.dot(
            keys_ref[:, step * deep : (step + 1) * deep],
            held_ref[step % SLOTS],
            preferred_element_type=jnp.float32,
        )
        if step + SLOTS < STEPS:
            copy(step + SLOTS).start()
        total = part if step == 0 else wide_ref[...] + part
        wide_ref[...] = total
        if step == STEPS - 1:
            sent_ref[...] = total.astype(sent_ref.dtype)


def product(keys, weights, span, wire, after):
    depth = weights.shape[0]
    rows, wide = keys.shape[0], span[1] - span[0]
    return pl.pallas_call(
        functools.partial(product_kernel, span[0]),
        in_specs=[VMEM, ANY, ANY],
        out_specs=[VMEM, VMEM],
        out_shape=[
            jax.ShapeDtypeStruct((rows, wide), jnp.float32),
            jax.ShapeDtypeStruct((rows, wide), wire),
        ],
        scratch_shapes=[
            pltpu.VMEM((SLOTS, depth // STEPS, wide), weights.dtype),
            pltpu.SemaphoreType.DMA((SLOTS,)),
        ],
        compiler_params=params(),
        cost_estimate=pl.CostEstimate(
            flops=2 * rows * depth * wide,
            bytes_accessed=2 * depth * (rows + wide) + 6 * rows * wide,
            transcendentals=0,
        ),
        name="product",
    )(keys, weights, after)


def add_kernel(wide_ref, came_ref, after_ref, total_ref, sent_ref):
    total = wide_ref[...] + came_ref[...].astype(jnp.float32)
    total_ref[...] = total
    sent_ref[...] = total.astype(sent_ref.dtype)


def added(wide, came, wire, after):
    return pl.pallas_call(
        add_kernel,
        in_specs=[VMEM, VMEM, ANY],
        out_specs=[VMEM, VMEM],
        out_shape=[jax.ShapeDtypeStruct(wide.shape, jnp.float32), jax.ShapeDtypeStruct(wide.shape, wire)],
        compiler_params=params(),
        name="added",
    )(wide, came, after)


def final_kernel(wide_ref, came_ref, after_ref, final_ref):
    final_ref[...] = (wide_ref[...] + came_ref[...].astype(jnp.float32)).astype(final_ref.dtype)


def finished(wide, came, after):
    return pl.pallas_call(
        final_kernel,
        in_specs=[VMEM, VMEM, ANY],
        out_specs=VMEM,
        out_shape=jax.ShapeDtypeStruct(wide.shape, jnp.bfloat16),
        compiler_params=params(),
        name="finished",
    )(wide, came, after)


def contract_kernel(span, done, at_ref, final_ref, came_ref, stored_ref, after_ref, *refs):
    before = refs[: done[0]]
    pieces = refs[done[0] : done[0] + done[1]]
    terms_ref, whitened_ref, rows_ref = refs[-3:]
    start = at_ref[1]

    @pl.when(at_ref[0] != 0)
    def _():
        rows_ref[...] = final_ref[...]

    @pl.when(at_ref[0] == 0)
    def _():
        rows_ref[...] = came_ref[...]

    batches, slots, _ = stored_ref.shape
    wide = span[1] - span[0]
    term = lax.dot_general(
        rows_ref[...],
        stored_ref[:, :, span[0] : span[1]].reshape(batches * slots, wide),
        (((1,), (1,)), ((), ())),
        preferred_element_type=jnp.float32,
    )
    terms_ref[...] = before[0][...] + term if before else term
    block = whitened_ref.shape[0]
    left = 0
    for piece in pieces:
        whitened_ref[:, left : left + piece.shape[1]] = piece[...]
        left += piece.shape[1]
    whitened_ref[:, left : left + wide] = rows_ref[pl.ds(pl.multiple_of(start, 16), block), :]


def contract(at, final, came, stored, terms, pieces, span, block, after):
    keys, wide = final.shape
    sums = stored.shape[0] * stored.shape[1]
    before = [] if terms is None else [terms]
    columns = wide + sum(p.shape[1] for p in pieces)
    return pl.pallas_call(
        functools.partial(contract_kernel, span, (len(before), len(pieces))),
        in_specs=[SMEM, VMEM, VMEM, VMEM, ANY] + [VMEM] * (len(before) + len(pieces)),
        out_specs=[VMEM, VMEM],
        out_shape=[
            jax.ShapeDtypeStruct((keys, sums), jnp.float32),
            jax.ShapeDtypeStruct((block, columns), jnp.bfloat16),
        ],
        scratch_shapes=[pltpu.VMEM((keys, wide), jnp.bfloat16)],
        compiler_params=params(),
        name="contract",
    )(at, final, came, stored, after, *before, *pieces)


def in_order(row_count, wire, inner, make, spans, close):
    half = row_count // 2
    count = len(spans)
    made, after = {}, None

    def sum_of(part, hop):
        nonlocal after
        wide, came = made[part]
        if hop < half - 1:
            wide, sent = added(wide, came, wire, after)
            after = sent
            made[part] = (wide, step_in(sent, hop + 1))
        elif hop == half - 1:
            final = finished(wide, came, after)
            after = final
            made[part] = (final, step_out(final, 0))
        else:
            final, came = made[part]
            final = jnp.where(inner[hop - half], final, came)
            made[part] = (final, step_out(final, hop - half + 1))

    def step_in(sent, hop):
        if hop == half - 1:
            pairs = [(half - 1, half), (half, half - 1)]
        else:
            pairs = [(hop, hop + 1), (row_count - 1 - hop, row_count - 2 - hop)]
        return lax.ppermute(sent, "row", pairs)

    def step_out(final, hop):
        low, high = half - 1 - hop, half + hop
        if low == 0:
            return final
        return lax.ppermute(final, "row", [(low, low - 1), (high, high + 1)])

    stages = 2 * half - 2
    for tick in range(count + stages + 2):
        for hop in range(stages):
            part = tick - 2 - hop
            if 0 <= part < count:
                sum_of(part, hop)
        if tick < count:
            wide, sent = make(tick, after)
            after = sent
            made[tick] = (wide, step_in(sent, 0))
        part = tick - 2 - stages
        if 0 <= part < count:
            after = close(part, *made[part], after)


def select_kernel(count, row_ref, batch_ref, used_ref, length_ref, slot_ref, *refs):
    parts, out_ref, held_ref = refs[:count], refs[count], refs[count + 1]
    batches, rows, slots = held_ref.shape[1:]
    for i, part in enumerate(parts):
        for b in range(batches):
            held_ref[i, b] = part[0, :, b * slots : (b + 1) * slots]
    row = row_ref[0]
    column = lax.broadcasted_iota(jnp.int32, (rows, slots), 1)
    for place in range(out_ref.shape[1]):
        batch = batch_ref[row, place]
        slot = slot_ref[batch]
        owner = lax.div(slot, batches)
        shift = lax.rem(row - owner + count, count)
        length = jnp.where(place < used_ref[row], length_ref[batch], 0)
        value = held_ref[shift, slot - owner * batches]
        out_ref[0, place] = jnp.where(column < length, value, 0.0)


def selected(parts, row_index, pair_batch, pair_count, batch_length, batch_slot, batches):
    count = len(parts)
    _, rows, wide = parts[0].shape
    slots = wide // batches
    places = pair_batch.shape[1]
    return pl.pallas_call(
        functools.partial(select_kernel, count),
        in_specs=[SMEM] * 5 + [VMEM] * count,
        out_specs=VMEM,
        out_shape=jax.ShapeDtypeStruct((1, places, rows, slots), jnp.float32),
        scratch_shapes=[pltpu.VMEM((count, batches, rows, slots), jnp.float32)],
        name="select",
    )(row_index[None], pair_batch, pair_count, batch_length, batch_slot, *parts)


def shards(new_keys, precision, stored_keys, pair_batch, pair_count, batch_length, batch_slot):
    row_count = lax.axis_size("row")
    col_count = lax.axis_size("col")
    row_index = lax.axis_index("row")
    col_index = lax.axis_index("col")
    total_keys = new_keys.shape[0] * col_count
    block = total_keys // row_count
    batches = stored_keys.shape[0]
    half = row_count // 2
    wire = jnp.bfloat16 if row_count <= 4 else jnp.float32

    away = jnp.where(row_index < half, half - 1 - row_index, row_index - half)
    inner = [away <= hop for hop in range(half)]
    at = jnp.stack([(away < half - 1).astype(jnp.int32), row_index * block])

    pieces, starts = gathered(new_keys, col_count, col_index)
    keys = assembled(pieces, jnp.stack(starts), total_keys)
    spans = ranges(precision.shape[1])
    whitened = []
    terms = None

    def make(part, after):
        return product(keys, precision, spans[part], wire, at if after is None else after)

    def close(part, final, came, after):
        nonlocal terms
        before = whitened if part == len(spans) - 1 else []
        terms, rows = contract(at, final, came, stored_keys, terms, before, spans[part], block, after)
        whitened.append(rows)
        return rows

    in_order(row_count, wire, inner, make, spans, close)

    share = block // col_count
    sums = terms.reshape(row_count, col_count, share, terms.shape[1])
    bit = 1
    while bit < col_count:
        if col_count == 8 and bit == 2:
            other = [lax.dynamic_index_in_dim(sums, (col_index // 2) ^ f, 1, keepdims=False) for f in range(4)]
            sums = other[0] + sum(flipped(other[f], 2 * f, col_count) for f in (3, 2, 1))
            sums = sums[:, None]
            break
        pairs = sums.reshape(row_count, sums.shape[1] // 2, 2, share, sums.shape[3])
        mine = (col_index // bit) % 2
        kept = lax.dynamic_index_in_dim(pairs, mine, 2, keepdims=False)
        left = lax.dynamic_index_in_dim(pairs, 1 - mine, 2, keepdims=False)
        sums = kept + flipped(left, bit, col_count)
        bit *= 2
    sums = sums[:, 0]
    parts = []
    for shift in range(row_count):
        part = lax.dynamic_slice_in_dim(sums, (row_index + shift) % row_count, 1, 0)
        if shift:
            part = lax.ppermute(part, "row", [(r, (r + shift) % row_count) for r in range(row_count)])
        parts.append(part)
    shares = selected(parts, row_index, pair_batch, pair_count, batch_length, batch_slot, batches)
    return (whitened[-1], shares)


def solution(mesh):
    placed = (P("col", "row"), P("row", "col"), P("row", None, "col"), P(), P(), P(), P())
    return jax.shard_map(
        shards,
        mesh=mesh,
        in_specs=placed,
        out_specs=(P("row", "col"), P("row", None, "col", None)),
        check_vma=False,
    )
```

```python
import functools

import jax
import jax.numpy as jnp
from jax import lax
from jax.experimental import pallas as pl
from jax.experimental.pallas import tpu as pltpu
from jax.sharding import PartitionSpec as P

PARTS = 5
STEPS = 7
SLOTS = 4
HOP = 8 * 2**20
PIECES = 4
EARLY = ((0,), (1,))
LANES = 128
VMEM = pl.BlockSpec(memory_space=pltpu.VMEM)
ANY = pl.BlockSpec(memory_space=pl.ANY)
SMEM = pl.BlockSpec(memory_space=pltpu.SMEM)


def flipped(array, bit, count):
    return lax.ppermute(array, "col", [(c, c ^ bit) for c in range(count)])


def gathered(new_keys, col_count, col_index, fetch):
    rows = new_keys.shape[0]
    if col_count != 8:
        return [new_keys, lax.all_gather(new_keys, "col", axis=0, tiled=True)], [jnp.int32(0)] * 2, new_keys
    half = rows // 2
    by_x = flipped(new_keys, 2, 8)
    by_y = flipped(new_keys, 4, 8)
    by_core = flipped(new_keys, 1, 8)
    after = fetch(0, by_core)
    low, high = halved(by_x, by_y, after)
    after = fetch(1, low)
    low = flipped(low, 4, 8)
    high = flipped(high, 2, 8)
    x_core = flipped(by_x, 1, 8)
    y_core = flipped(by_y, 1, 8)
    low_core = flipped(low, 1, 8)
    high_core = flipped(high, 1, 8)
    pieces = [new_keys, by_core, by_x, x_core, by_y, y_core, low, high, low_core, high_core]
    of = [0, 1, 2, 3, 4, 5, 6, 6, 7, 7]
    within = [0] * 7 + [half, 0, half]
    return pieces, [(col_index ^ f) * rows + w for f, w in zip(of, within)], after


def halved_kernel(x_ref, y_ref, after_ref, low_ref, high_ref):
    half = low_ref.shape[0]
    low_ref[...] = x_ref[:half]
    high_ref[...] = y_ref[half:]


def halved(by_x, by_y, after):
    rows, depth = by_x.shape
    return pl.pallas_call(
        halved_kernel,
        in_specs=[VMEM, VMEM, ANY],
        out_specs=[VMEM, VMEM],
        out_shape=[jax.ShapeDtypeStruct((rows // 2, depth), by_x.dtype)] * 2,
        compiler_params=params(),
        cost_estimate=cost(),
        name="halved",
    )(by_x, by_y, after)


def fetch_kernel(spans, weights_ref, after_ref, *refs):
    token_ref, arrived = refs[-2:]
    token_ref[...] = jnp.zeros_like(token_ref)
    copies = []
    for i, (span, ref) in enumerate(zip(spans, refs[:-2])):
        deep = ref.shape[0] // PIECES
        for k in range(PIECES):
            rows = pl.ds(k * deep, deep)
            source = weights_ref.at[rows, pl.ds(span[0], span[1] - span[0])]
            copies.append(pltpu.make_async_copy(source, ref.at[rows, :], arrived.at[i * PIECES + k]))
    for copy in copies:
        copy.start()
    for copy in copies:
        copy.wait()


def fetched(weights, spans, after):
    depth = weights.shape[0]
    return pl.pallas_call(
        functools.partial(fetch_kernel, spans),
        in_specs=[ANY, ANY],
        out_specs=[VMEM] * (len(spans) + 1),
        out_shape=[jax.ShapeDtypeStruct((depth, e - b), weights.dtype) for b, e in spans]
        + [jax.ShapeDtypeStruct((8, LANES), jnp.float32)],
        scratch_shapes=[pltpu.SemaphoreType.DMA((PIECES * len(spans),))],
        compiler_params=params(),
        cost_estimate=cost(),
        name="fetch",
    )(weights, after)


def ranges(columns):
    tiles = columns // LANES
    count = min(PARTS, tiles)
    ends = [(tiles * (i + 1) + count // 2) // count * LANES for i in range(count)]
    return list(zip([0] + ends[:-1], ends))


def cost(size=1):
    return pl.CostEstimate(flops=1, bytes_accessed=size, transcendentals=0)


def params():
    return pltpu.CompilerParams(vmem_limit_bytes=12 * 2**20)


def assemble_kernel(count, starts_ref, after_ref, own_ref, *refs):
    pieces, keys_ref, arrived = refs[:count], refs[count], refs[count + 1]
    own = pl.ds(pl.multiple_of(starts_ref[0], 16), own_ref.shape[0])
    copy = pltpu.make_async_copy(own_ref, keys_ref.at[own, :], arrived)
    copy.start()
    copy.wait()
    for i, piece in enumerate(pieces):
        keys_ref[pl.ds(pl.multiple_of(starts_ref[i + 1], 16), piece.shape[0]), :] = piece[...]


def assembled(pieces, starts, keys, after):
    return pl.pallas_call(
        functools.partial(assemble_kernel, len(pieces) - 1),
        in_specs=[SMEM, ANY, ANY] + [VMEM] * (len(pieces) - 1),
        out_specs=VMEM,
        out_shape=jax.ShapeDtypeStruct((keys, pieces[0].shape[1]), pieces[0].dtype),
        scratch_shapes=[pltpu.SemaphoreType.DMA],
        compiler_params=params(),
        cost_estimate=cost(),
        name="assemble",
    )(starts, after, *pieces)


def product_kernel(left, early, keys_ref, weights_ref, stored_ref, after_ref, *refs):
    wide_ref, sent_ref, columns_ref, held_ref, arrived = refs
    wide = wide_ref.shape[1]
    deep = keys_ref.shape[1] // STEPS

    def copy(step):
        return pltpu.make_async_copy(
            weights_ref.at[pl.ds(step * deep, deep), pl.ds(left, wide)],
            held_ref.at[step % SLOTS],
            arrived.at[step % SLOTS],
        )

    other = pltpu.make_async_copy(stored_ref.at[:, :, pl.ds(left, wide)], columns_ref, arrived.at[SLOTS])
    if not early:
        for step in range(min(SLOTS, STEPS)):
            copy(step).start()
    other.start()
    for step in range(STEPS):
        if early:
            weights = weights_ref[step * deep : (step + 1) * deep, :]
        else:
            copy(step).wait()
            weights = held_ref[step % SLOTS]
        part = jnp.dot(
            keys_ref[:, step * deep : (step + 1) * deep],
            weights,
            preferred_element_type=jnp.float32,
        )
        if not early and step + SLOTS < STEPS:
            copy(step + SLOTS).start()
        total = part if step == 0 else wide_ref[...] + part
        wide_ref[...] = total
        if step == STEPS - 1:
            sent_ref[...] = total.astype(sent_ref.dtype)
    other.wait()


def product(keys, weights, early, stored, span, wire, after):
    depth = weights.shape[0]
    rows, wide = keys.shape[0], span[1] - span[0]
    return pl.pallas_call(
        functools.partial(product_kernel, span[0], early),
        in_specs=[VMEM, VMEM if early else ANY, ANY, ANY],
        out_specs=[VMEM, VMEM, VMEM],
        out_shape=[
            jax.ShapeDtypeStruct((rows, wide), jnp.float32),
            jax.ShapeDtypeStruct((rows, wide), wire),
            jax.ShapeDtypeStruct(stored.shape[:2] + (wide,), stored.dtype),
        ],
        scratch_shapes=[
            pltpu.VMEM((SLOTS, 16 if early else depth // STEPS, wide), weights.dtype),
            pltpu.SemaphoreType.DMA((SLOTS + 1,)),
        ],
        compiler_params=params(),
        cost_estimate=cost(),
        name="product",
    )(keys, weights, stored, after)


def add_kernel(wide_ref, came_ref, after_ref, total_ref, sent_ref):
    total = wide_ref[...] + came_ref[...].astype(jnp.float32)
    total_ref[...] = total
    sent_ref[...] = total.astype(sent_ref.dtype)


def added(wide, came, wire, after):
    return pl.pallas_call(
        add_kernel,
        in_specs=[VMEM, VMEM, ANY],
        out_specs=[VMEM, VMEM],
        out_shape=[jax.ShapeDtypeStruct(wide.shape, jnp.float32), jax.ShapeDtypeStruct(wide.shape, wire)],
        compiler_params=params(),
        cost_estimate=cost(HOP),
        name="added",
    )(wide, came, after)


def final_kernel(wide_ref, came_ref, after_ref, final_ref):
    final_ref[...] = (wide_ref[...] + came_ref[...].astype(jnp.float32)).astype(final_ref.dtype)


def finished(wide, came, after):
    return pl.pallas_call(
        final_kernel,
        in_specs=[VMEM, VMEM, ANY],
        out_specs=VMEM,
        out_shape=jax.ShapeDtypeStruct(wide.shape, jnp.bfloat16),
        compiler_params=params(),
        cost_estimate=cost(HOP),
        name="finished",
    )(wide, came, after)


def contract_kernel(done, at_ref, final_ref, came_ref, stored_ref, after_ref, *refs):
    before = refs[: done[0]]
    pieces = refs[done[0] : done[0] + done[1]]
    terms_ref, whitened_ref, rows_ref = refs[-3:]
    start = at_ref[1]

    @pl.when(at_ref[0] != 0)
    def _():
        rows_ref[...] = final_ref[...]

    @pl.when(at_ref[0] == 0)
    def _():
        rows_ref[...] = came_ref[...]

    batches, slots, wide = stored_ref.shape
    term = lax.dot_general(
        rows_ref[...],
        stored_ref[...].reshape(batches * slots, wide),
        (((1,), (1,)), ((), ())),
        preferred_element_type=jnp.float32,
    )
    terms_ref[...] = before[0][...] + term if before else term
    block = whitened_ref.shape[0]
    left = 0
    for piece in pieces:
        whitened_ref[:, left : left + piece.shape[1]] = piece[...]
        left += piece.shape[1]
    whitened_ref[:, left : left + wide] = rows_ref[pl.ds(pl.multiple_of(start, 16), block), :]


def contract(at, final, came, stored, terms, pieces, block, after):
    keys, wide = final.shape
    sums = stored.shape[0] * stored.shape[1]
    before = [] if terms is None else [terms]
    columns = wide + sum(p.shape[1] for p in pieces)
    return pl.pallas_call(
        functools.partial(contract_kernel, (len(before), len(pieces))),
        in_specs=[SMEM, VMEM, VMEM, VMEM, ANY] + [VMEM] * (len(before) + len(pieces)),
        out_specs=[VMEM, VMEM],
        out_shape=[
            jax.ShapeDtypeStruct((keys, sums), jnp.float32),
            jax.ShapeDtypeStruct((block, columns), jnp.bfloat16),
        ],
        scratch_shapes=[pltpu.VMEM((keys, wide), jnp.bfloat16)],
        compiler_params=params(),
        cost_estimate=cost(HOP),
        name="contract",
    )(at, final, came, stored, after, *before, *pieces)


def in_order(row_count, wire, inner, make, spans, close):
    half = row_count // 2
    count = len(spans)
    made, after = {}, None

    def sum_of(part, hop):
        nonlocal after
        wide, came = made[part]
        if hop < half - 1:
            wide, sent = added(wide, came, wire, after)
            after = sent
            made[part] = (wide, step_in(sent, hop + 1))
        elif hop == half - 1:
            final = finished(wide, came, after)
            after = final
            made[part] = (final, step_out(final, 0))
        else:
            final, came = made[part]
            final = jnp.where(inner[hop - half], final, came)
            made[part] = (final, step_out(final, hop - half + 1))

    def step_in(sent, hop):
        if hop == half - 1:
            pairs = [(half - 1, half), (half, half - 1)]
        else:
            pairs = [(hop, hop + 1), (row_count - 1 - hop, row_count - 2 - hop)]
        return lax.ppermute(sent, "row", pairs)

    def step_out(final, hop):
        low, high = half - 1 - hop, half + hop
        if low == 0:
            return final
        return lax.ppermute(final, "row", [(low, low - 1), (high, high + 1)])

    stages = 2 * half - 2
    for tick in range(count + stages + 2):
        for hop in range(stages):
            part = tick - 2 - hop
            if 0 <= part < count:
                sum_of(part, hop)
        if tick < count:
            wide, sent = make(tick, after)
            after = sent
            made[tick] = (wide, step_in(sent, 0))
        part = tick - 2 - stages
        if 0 <= part < count:
            after = close(part, *made[part], after)


def select_kernel(count, row_ref, batch_ref, used_ref, length_ref, slot_ref, *refs):
    parts, out_ref, held_ref = refs[:count], refs[count], refs[count + 1]
    batches, rows, slots = held_ref.shape[1:]
    for i, part in enumerate(parts):
        for b in range(batches):
            held_ref[i, b] = part[0, :, b * slots : (b + 1) * slots]
    row = row_ref[0]
    column = lax.broadcasted_iota(jnp.int32, (rows, slots), 1)
    for place in range(out_ref.shape[1]):
        batch = batch_ref[row, place]
        slot = slot_ref[batch]
        owner = lax.div(slot, batches)
        shift = lax.rem(row - owner + count, count)
        length = jnp.where(place < used_ref[row], length_ref[batch], 0)
        value = held_ref[shift, slot - owner * batches]
        out_ref[0, place] = jnp.where(column < length, value, 0.0)


def selected(parts, row_index, pair_batch, pair_count, batch_length, batch_slot, batches):
    count = len(parts)
    _, rows, wide = parts[0].shape
    slots = wide // batches
    places = pair_batch.shape[1]
    return pl.pallas_call(
        functools.partial(select_kernel, count),
        in_specs=[SMEM] * 5 + [VMEM] * count,
        out_specs=VMEM,
        out_shape=jax.ShapeDtypeStruct((1, places, rows, slots), jnp.float32),
        scratch_shapes=[pltpu.VMEM((count, batches, rows, slots), jnp.float32)],
        cost_estimate=cost(),
        name="select",
    )(row_index[None], pair_batch, pair_count, batch_length, batch_slot, *parts)


def shards(new_keys, precision, stored_keys, pair_batch, pair_count, batch_length, batch_slot):
    row_count = lax.axis_size("row")
    col_count = lax.axis_size("col")
    row_index = lax.axis_index("row")
    col_index = lax.axis_index("col")
    total_keys = new_keys.shape[0] * col_count
    block = total_keys // row_count
    batches = stored_keys.shape[0]
    half = row_count // 2
    wire = jnp.bfloat16 if row_count <= 4 else jnp.float32

    away = jnp.where(row_index < half, half - 1 - row_index, row_index - half)
    inner = [away <= hop for hop in range(half)]
    at = jnp.stack([(away < half - 1).astype(jnp.int32), row_index * block])

    spans = ranges(precision.shape[1])
    early = {}

    def fetch(turn, after):
        parts = [p for p in EARLY[turn] if p < len(spans)]
        *held, token = fetched(precision, [spans[p] for p in parts], after)
        early.update(zip(parts, held))
        return token

    pieces, starts, after = gathered(new_keys, col_count, col_index, fetch)
    keys = assembled(pieces, jnp.stack(starts), total_keys, after)
    whitened = []
    columns = []
    terms = None

    def make(part, after):
        weights = early.get(part, precision)
        after = at if after is None else after
        *made, held = product(keys, weights, part in early, stored_keys, spans[part], wire, after)
        columns.append(held)
        return made

    def close(part, final, came, after):
        nonlocal terms
        before = whitened if part == len(spans) - 1 else []
        terms, rows = contract(at, final, came, columns[part], terms, before, block, after)
        whitened.append(rows)
        return rows

    in_order(row_count, wire, inner, make, spans, close)

    share = block // col_count
    sums = terms.reshape(row_count, col_count, share, terms.shape[1])
    bit = 1
    while bit < col_count:
        if col_count == 8 and bit == 2:
            other = [lax.dynamic_index_in_dim(sums, (col_index // 2) ^ f, 1, keepdims=False) for f in range(4)]
            sums = other[0] + sum(flipped(other[f], 2 * f, col_count) for f in (3, 2, 1))
            sums = sums[:, None]
            break
        pairs = sums.reshape(row_count, sums.shape[1] // 2, 2, share, sums.shape[3])
        mine = (col_index // bit) % 2
        kept = lax.dynamic_index_in_dim(pairs, mine, 2, keepdims=False)
        left = lax.dynamic_index_in_dim(pairs, 1 - mine, 2, keepdims=False)
        sums = kept + flipped(left, bit, col_count)
        bit *= 2
    sums = sums[:, 0]
    parts = []
    for shift in range(row_count):
        part = lax.dynamic_slice_in_dim(sums, (row_index + shift) % row_count, 1, 0)
        if shift:
            part = lax.ppermute(part, "row", [(r, (r + shift) % row_count) for r in range(row_count)])
        parts.append(part)
    shares = selected(parts, row_index, pair_batch, pair_count, batch_length, batch_slot, batches)
    return (whitened[-1], shares)


def solution(mesh):
    placed = (P("col", "row"), P("row", "col"), P("row", None, "col"), P(), P(), P(), P())
    return jax.shard_map(
        shards,
        mesh=mesh,
        in_specs=placed,
        out_specs=(P("row", "col"), P("row", None, "col", None)),
        check_vma=False,
    )
```

```python
import functools

import jax
import jax.numpy as jnp
from jax import lax
from jax.experimental import pallas as pl
from jax.experimental.pallas import tpu as pltpu
from jax.sharding import PartitionSpec as P

PARTS = 4
STEPS = 7
SLOTS = 4
PIECES = 4
LANES = 128
VMEM = pl.BlockSpec(memory_space=pltpu.VMEM)
ANY = pl.BlockSpec(memory_space=pl.ANY)
SMEM = pl.BlockSpec(memory_space=pltpu.SMEM)


def flipped(array, bit, count):
    return lax.ppermute(array, "col", [(c, c ^ bit) for c in range(count)])


def gathered(new_keys, col_count, col_index, fetch):
    rows = new_keys.shape[0]
    if col_count != 8:
        own, after = fetch(new_keys)
        start = col_index * rows
        return [own, lax.all_gather(new_keys, "col", axis=0, tiled=True)], [start, jnp.int32(0)], after
    half = rows // 2
    by_x = flipped(new_keys, 2, 8)
    by_y = flipped(new_keys, 4, 8)
    by_core = flipped(new_keys, 1, 8)
    own, after = fetch(by_core)
    low, high = halved(by_x, by_y, after)
    low = flipped(low, 4, 8)
    high = flipped(high, 2, 8)
    x_core = flipped(by_x, 1, 8)
    y_core = flipped(by_y, 1, 8)
    low_core = flipped(low, 1, 8)
    high_core = flipped(high, 1, 8)
    pieces = [own, by_core, by_x, x_core, by_y, y_core, low, high, low_core, high_core]
    of = [0, 1, 2, 3, 4, 5, 6, 6, 7, 7]
    within = [0] * 7 + [half, 0, half]
    return pieces, [(col_index ^ f) * rows + w for f, w in zip(of, within)], after


def halved_kernel(x_ref, y_ref, after_ref, low_ref, high_ref):
    half = low_ref.shape[0]
    low_ref[...] = x_ref[:half]
    high_ref[...] = y_ref[half:]


def halved(by_x, by_y, after):
    rows, depth = by_x.shape
    return pl.pallas_call(
        halved_kernel,
        in_specs=[VMEM, VMEM, ANY],
        out_specs=[VMEM, VMEM],
        out_shape=[jax.ShapeDtypeStruct((rows // 2, depth), by_x.dtype)] * 2,
        compiler_params=params(),
        cost_estimate=cost(),
        name="halved",
    )(by_x, by_y, after)


def fetch_kernel(span, weights_ref, stored_ref, own_ref, after_ref, held_ref, batches_ref, keys_ref, token_ref, arrived):
    deep = held_ref.shape[0] // PIECES
    copies = [
        pltpu.make_async_copy(own_ref, keys_ref, arrived.at[PIECES]),
        pltpu.make_async_copy(stored_ref, batches_ref, arrived.at[PIECES + 1]),
    ]
    for k in range(PIECES):
        rows = pl.ds(k * deep, deep)
        source = weights_ref.at[rows, pl.ds(span[0], span[1] - span[0])]
        copies.append(pltpu.make_async_copy(source, held_ref.at[rows, :], arrived.at[k]))
    for copy in copies:
        copy.start()
    token_ref[...] = jnp.zeros_like(token_ref)
    for copy in copies:
        copy.wait()


def fetched(weights, stored, own, span, after):
    depth, wide = weights.shape[0], span[1] - span[0]
    return pl.pallas_call(
        functools.partial(fetch_kernel, span),
        in_specs=[ANY] * 4,
        out_specs=[VMEM] * 4,
        out_shape=[
            jax.ShapeDtypeStruct((depth, wide), weights.dtype),
            jax.ShapeDtypeStruct(stored.shape, stored.dtype),
            jax.ShapeDtypeStruct(own.shape, own.dtype),
            jax.ShapeDtypeStruct((8, LANES), jnp.float32),
        ],
        scratch_shapes=[pltpu.SemaphoreType.DMA((PIECES + 2,))],
        compiler_params=params(),
        cost_estimate=cost(),
        name="fetch",
    )(weights, stored, own, after)


def ranges(columns):
    tiles = columns // LANES
    count = max(n for n in range(1, PARTS + 1) if tiles % n == 0)
    wide = tiles // count * LANES
    return [(i * wide, (i + 1) * wide) for i in range(count)]


def cost():
    return pl.CostEstimate(flops=1, bytes_accessed=1, transcendentals=0)


def params():
    return pltpu.CompilerParams(vmem_limit_bytes=12 * 2**20)


def assemble_kernel(count, starts_ref, after_ref, *refs):
    keys_ref = refs[count]
    for i, piece in enumerate(refs[:count]):
        keys_ref[pl.ds(pl.multiple_of(starts_ref[i], 16), piece.shape[0]), :] = piece[...]


def assembled(pieces, starts, keys, after):
    return pl.pallas_call(
        functools.partial(assemble_kernel, len(pieces)),
        in_specs=[SMEM, ANY] + [VMEM] * len(pieces),
        out_specs=VMEM,
        out_shape=jax.ShapeDtypeStruct((keys, pieces[0].shape[1]), pieces[0].dtype),
        compiler_params=params(),
        cost_estimate=cost(),
        name="assemble",
    )(starts, after, *pieces)


def multiply(left, early, keys_ref, weights_ref, wide_ref, held_ref, arrived):
    wide = wide_ref.shape[1]
    deep = keys_ref.shape[1] // STEPS

    def copy(step):
        return pltpu.make_async_copy(
            weights_ref.at[pl.ds(step * deep, deep), pl.ds(left, wide)],
            held_ref.at[step % SLOTS],
            arrived.at[step % SLOTS],
        )

    if not early:
        for step in range(min(SLOTS, STEPS)):
            copy(step).start()
    for step in range(STEPS):
        if early:
            weights = weights_ref[step * deep : (step + 1) * deep, :]
        else:
            copy(step).wait()
            weights = held_ref[step % SLOTS]
        part = jnp.dot(
            keys_ref[:, step * deep : (step + 1) * deep],
            weights,
            preferred_element_type=jnp.float32,
        )
        if not early and step + SLOTS < STEPS:
            copy(step + SLOTS).start()
        wide_ref[...] = part if step == 0 else wide_ref[...] + part


def against(left, at_ref, final_ref, came_ref, stored_ref, before, terms_ref, piece_ref, rows_ref):
    @pl.when(at_ref[0] != 0)
    def _():
        rows_ref[...] = final_ref[...]

    @pl.when(at_ref[0] == 0)
    def _():
        rows_ref[...] = came_ref[...]

    batches, slots, _ = stored_ref.shape
    wide = rows_ref.shape[1]
    term = lax.dot_general(
        rows_ref[...],
        stored_ref[:, :, left : left + wide].reshape(batches * slots, wide),
        (((1,), (1,)), ((), ())),
        preferred_element_type=jnp.float32,
    )
    terms_ref[...] = before[0][...] + term if before else term
    piece_ref[...] = rows_ref[pl.ds(pl.multiple_of(at_ref[1], 16), piece_ref.shape[0]), :]


def work_kernel(product, contract, joined, at_ref, after_ref, *refs):
    refs = list(refs)
    take = lambda n: [refs.pop(0) for _ in range(n)]
    if product:
        factors = take(2)
    if contract:
        rows = take(3)
        before = take(contract[1])
        pieces = take(joined)
    if product:
        (wide_ref,) = take(1)
    if contract:
        terms_ref, piece_ref = take(2)
    if joined:
        (whole_ref,) = take(1)
    if product:
        multiply(*product, *factors, wide_ref, *take(2))
    if contract:
        against(contract[0], at_ref, *rows, before, terms_ref, piece_ref, *take(1))
    if joined:
        left = 0
        for piece in pieces + [piece_ref]:
            whole_ref[:, left : left + piece.shape[1]] = piece[...]
            left += piece.shape[1]


def work(at, after, product=None, contract=None, pieces=()):
    operands, specs, shapes, scratch = [at, after], [SMEM, ANY], [], []
    product_at = contract_at = None
    if product:
        keys, weights, early, span = product
        depth, rows, wide = weights.shape[0], keys.shape[0], span[1] - span[0]
        product_at = (span[0], early)
        operands += [keys, weights]
        specs += [VMEM, VMEM if early else ANY]
        shapes += [jax.ShapeDtypeStruct((rows, wide), jnp.float32)]
        scratch += [
            pltpu.VMEM((SLOTS, 16 if early else depth // STEPS, wide), weights.dtype),
            pltpu.SemaphoreType.DMA((SLOTS,)),
        ]
    if contract:
        final, came, stored, terms, left, block = contract
        rows, wide = final.shape
        before = [] if terms is None else [terms]
        contract_at = (left, len(before))
        operands += [final, came, stored, *before, *pieces]
        specs += [VMEM] * (3 + len(before) + len(pieces))
        shapes += [
            jax.ShapeDtypeStruct((rows, stored.shape[0] * stored.shape[1]), jnp.float32),
            jax.ShapeDtypeStruct((block, wide), jnp.bfloat16),
        ]
        scratch += [pltpu.VMEM((rows, wide), jnp.bfloat16)]
    if pieces:
        columns = sum(p.shape[1] for p in pieces) + wide
        shapes += [jax.ShapeDtypeStruct((block, columns), jnp.bfloat16)]
    return pl.pallas_call(
        functools.partial(work_kernel, product_at, contract_at, len(pieces)),
        in_specs=specs,
        out_specs=[VMEM] * len(shapes),
        out_shape=shapes,
        scratch_shapes=scratch,
        compiler_params=params(),
        cost_estimate=cost(),
        name="work",
    )(*operands)


def tick_kernel(names, outs, at_ref, after_ref, *refs):
    given = dict(zip(names, refs))
    made = dict(zip(outs, refs[len(names) :]))
    if "total" in made:
        total = given["wide"][...] + given["outer"][...].astype(jnp.float32)
        made["total"][...] = total
        made["across"][...] = total.astype(jnp.bfloat16)
    if "final" in made:
        final = (given["held"][...] + given["middle"][...].astype(jnp.float32)).astype(jnp.bfloat16)
        made["final"][...] = final
    if "along" in made:
        along = given["next"][...].astype(jnp.bfloat16)
        if "final" in made:
            along = jnp.where(at_ref[0] != 0, final, along)
        made["along"][...] = along


def tick(at, after, outs, **given):
    shape = next(iter(given.values())).shape
    wide = {"total": jnp.float32}
    made = pl.pallas_call(
        functools.partial(tick_kernel, tuple(given), outs),
        in_specs=[SMEM, ANY] + [VMEM] * len(given),
        out_specs=[VMEM] * len(outs),
        out_shape=[jax.ShapeDtypeStruct(shape, wide.get(name, jnp.bfloat16)) for name in outs],
        compiler_params=params(),
        cost_estimate=cost(),
        name="tick",
    )(at, after, *given.values())
    return dict(zip(outs, made))


def along_line(at, multiplied, contracted, count):
    wide, total, final = {}, {}, {}
    (wide[0],) = multiplied(0, at)
    outer = middle = None
    after = wide[0]
    for k in range(count + 2):
        outs, given = [], {}
        if 1 <= k <= count:
            outs += ["total", "across"]
            given.update(wide=wide[k - 1], outer=outer)
        if k >= 2:
            outs += ["final"]
            given.update(held=total[k - 2], middle=middle)
        if k < count:
            outs += ["along"]
            given.update(next=wide[k])
        made = tick(at, after, tuple(outs), **given)
        earlier = outer
        if k >= 2:
            final[k - 2] = made["final"]
        if 1 <= k <= count:
            total[k - 1] = made["total"]
            middle = lax.ppermute(made["across"], "row", [(1, 2), (2, 1)])
        pairs = ([(0, 1), (3, 2)] if k < count else []) + ([(1, 0), (2, 3)] if k >= 2 else [])
        sent = made["along"] if k < count else made["final"] if k >= 2 else made["across"]
        if pairs:
            outer = lax.ppermute(sent, "row", pairs)
        after = sent
        if k + 1 < count or k >= 3:
            product = k + 1 if k + 1 < count else None
            contract = (k - 3, final[k - 3], earlier) if k >= 3 else None
            out = multiplied(product, after, contract)
            if product is not None:
                wide[product] = out[0]
            after = out[-1]
    contracted(count - 1, final[count - 1], outer, after)


def select_kernel(count, row_ref, batch_ref, used_ref, length_ref, slot_ref, *refs):
    parts, out_ref, held_ref = refs[:count], refs[count], refs[count + 1]
    batches, rows, slots = held_ref.shape[1:]
    for i, part in enumerate(parts):
        for b in range(batches):
            held_ref[i, b] = part[0, :, b * slots : (b + 1) * slots]
    row = row_ref[0]
    column = lax.broadcasted_iota(jnp.int32, (rows, slots), 1)
    for place in range(out_ref.shape[1]):
        batch = batch_ref[row, place]
        slot = slot_ref[batch]
        owner = lax.div(slot, batches)
        shift = lax.rem(row - owner + count, count)
        length = jnp.where(place < used_ref[row], length_ref[batch], 0)
        value = held_ref[shift, slot - owner * batches]
        out_ref[0, place] = jnp.where(column < length, value, 0.0)


def selected(parts, row_index, pair_batch, pair_count, batch_length, batch_slot, batches):
    count = len(parts)
    _, rows, wide = parts[0].shape
    slots = wide // batches
    places = pair_batch.shape[1]
    return pl.pallas_call(
        functools.partial(select_kernel, count),
        in_specs=[SMEM] * 5 + [VMEM] * count,
        out_specs=VMEM,
        out_shape=jax.ShapeDtypeStruct((1, places, rows, slots), jnp.float32),
        scratch_shapes=[pltpu.VMEM((count, batches, rows, slots), jnp.float32)],
        cost_estimate=cost(),
        name="select",
    )(row_index[None], pair_batch, pair_count, batch_length, batch_slot, *parts)


def shards(new_keys, precision, stored_keys, pair_batch, pair_count, batch_length, batch_slot):
    row_count = lax.axis_size("row")
    col_count = lax.axis_size("col")
    row_index = lax.axis_index("row")
    col_index = lax.axis_index("col")
    total_keys = new_keys.shape[0] * col_count
    block = total_keys // row_count
    batches = stored_keys.shape[0]
    half = row_count // 2

    away = jnp.where(row_index < half, half - 1 - row_index, row_index - half)
    at = jnp.stack([(away == 0).astype(jnp.int32), row_index * block])
    spans = ranges(precision.shape[1])
    count = len(spans)
    early, stored, own, token = None, None, None, None

    def fetch(after):
        nonlocal early, stored, token
        early, stored, own, token = fetched(precision, stored_keys, new_keys, spans[0], after)
        return own, token

    pieces, starts, token = gathered(new_keys, col_count, col_index, fetch)
    order = list(range(1, len(pieces))) + [0]
    keys = assembled([pieces[i] for i in order], jnp.stack([starts[i] for i in order]), total_keys, token)
    terms = None
    whitened = []

    def multiplied(part, after, contract=None):
        nonlocal terms
        product = None
        if part is not None:
            product = (keys, precision if part else early, part == 0, spans[part])
        if contract is not None:
            number, final, came = contract
            contract = (final, came, stored, terms, spans[number][0], block)
        joined = whitened if contract is not None and number == count - 1 else []
        out = work(at, after, product, contract, joined)
        if contract is not None:
            first = 1 if product else 0
            terms = out[first]
            whitened.append(out[-1])
        return out

    def contracted(part, final, came, after):
        multiplied(None, after, (part, final, came))

    if row_count == 4:
        along_line(at, multiplied, contracted, count)
    else:
        after = at
        for part in range(count):
            (wide,) = multiplied(part, after)
            every = lax.psum(wide, "row").astype(jnp.bfloat16)
            contracted(part, every, every, wide)
            after = whitened[-1]

    share = block // col_count
    sums = terms.reshape(row_count, col_count, share, terms.shape[1])
    bit = 1
    while bit < col_count:
        if col_count == 8 and bit == 2:
            other = [lax.dynamic_index_in_dim(sums, (col_index // 2) ^ f, 1, keepdims=False) for f in range(4)]
            sums = other[0] + sum(flipped(other[f], 2 * f, col_count) for f in (3, 2, 1))
            sums = sums[:, None]
            break
        pairs = sums.reshape(row_count, sums.shape[1] // 2, 2, share, sums.shape[3])
        mine = (col_index // bit) % 2
        kept = lax.dynamic_index_in_dim(pairs, mine, 2, keepdims=False)
        left = lax.dynamic_index_in_dim(pairs, 1 - mine, 2, keepdims=False)
        sums = kept + flipped(left, bit, col_count)
        bit *= 2
    sums = sums[:, 0]
    parts = []
    for shift in range(row_count):
        part = lax.dynamic_slice_in_dim(sums, (row_index + shift) % row_count, 1, 0)
        if shift:
            part = lax.ppermute(part, "row", [(r, (r + shift) % row_count) for r in range(row_count)])
        parts.append(part)
    shares = selected(parts, row_index, pair_batch, pair_count, batch_length, batch_slot, batches)
    return (whitened[-1], shares)


def solution(mesh):
    placed = (P("col", "row"), P("row", "col"), P("row", None, "col"), P(), P(), P(), P())
    return jax.shard_map(
        shards,
        mesh=mesh,
        in_specs=placed,
        out_specs=(P("row", "col"), P("row", None, "col", None)),
        check_vma=False,
    )
```

```python
import functools

import jax
import jax.numpy as jnp
from jax import lax
from jax.experimental import pallas as pl
from jax.experimental.pallas import tpu as pltpu
from jax.sharding import PartitionSpec as P

PARTS = 4
STEPS = 7
SLOTS = 4
AHEAD = 3
LANES = 128
VMEM = pl.BlockSpec(memory_space=pltpu.VMEM)
ANY = pl.BlockSpec(memory_space=pl.ANY)
SMEM = pl.BlockSpec(memory_space=pltpu.SMEM)


def flipped(array, bit, count):
    return lax.ppermute(array, "col", [(c, c ^ bit) for c in range(count)])


def gathered(new_keys, col_count, col_index, fetch):
    rows = new_keys.shape[0]
    if col_count != 8:
        after = fetch(new_keys)
        start = col_index * rows
        return [new_keys, lax.all_gather(new_keys, "col", axis=0, tiled=True)], [start, jnp.int32(0)], after
    half = rows // 2
    by_x = flipped(new_keys, 2, 8)
    by_y = flipped(new_keys, 4, 8)
    by_core = flipped(new_keys, 1, 8)
    after = fetch(by_core)
    low, high = halved(by_x, by_y, after)
    low = flipped(low, 4, 8)
    high = flipped(high, 2, 8)
    x_core = flipped(by_x, 1, 8)
    y_core = flipped(by_y, 1, 8)
    low_core = flipped(low, 1, 8)
    high_core = flipped(high, 1, 8)
    pieces = [new_keys, by_core, by_x, x_core, by_y, y_core, low, high, low_core, high_core]
    of = [0, 1, 2, 3, 4, 5, 6, 6, 7, 7]
    within = [0] * 7 + [half, 0, half]
    return pieces, [(col_index ^ f) * rows + w for f, w in zip(of, within)], after


def halved_kernel(x_ref, y_ref, after_ref, low_ref, high_ref):
    half = low_ref.shape[0]
    low_ref[...] = x_ref[:half]
    high_ref[...] = y_ref[half:]


def halved(by_x, by_y, after):
    rows, depth = by_x.shape
    return pl.pallas_call(
        halved_kernel,
        in_specs=[VMEM, VMEM, ANY],
        out_specs=[VMEM, VMEM],
        out_shape=[jax.ShapeDtypeStruct((rows // 2, depth), by_x.dtype)] * 2,
        compiler_params=params(),
        cost_estimate=cost(),
        name="halved",
    )(by_x, by_y, after)


def fetch_kernel(left, weights_ref, after_ref, held_ref, token_ref, arrived):
    deep = held_ref.shape[0] // AHEAD
    copies = []
    for k in range(AHEAD):
        rows = pl.ds(k * deep, deep)
        source = weights_ref.at[rows, pl.ds(left, held_ref.shape[1])]
        copies.append(pltpu.make_async_copy(source, held_ref.at[rows, :], arrived.at[k]))
    for copy in copies:
        copy.start()
    token_ref[...] = jnp.zeros_like(token_ref)
    for copy in copies:
        copy.wait()


def fetched(weights, span, after):
    return pl.pallas_call(
        functools.partial(fetch_kernel, span[0]),
        in_specs=[ANY] * 2,
        out_specs=[VMEM] * 2,
        out_shape=[
            jax.ShapeDtypeStruct((weights.shape[0] // STEPS * AHEAD, span[1] - span[0]), weights.dtype),
            jax.ShapeDtypeStruct((8, LANES), jnp.float32),
        ],
        scratch_shapes=[pltpu.SemaphoreType.DMA((AHEAD,))],
        compiler_params=params(),
        cost_estimate=cost(),
        name="fetch",
    )(weights, after)


def ranges(columns):
    tiles = columns // LANES
    count = max(n for n in range(1, PARTS + 1) if tiles % n == 0)
    wide = tiles // count * LANES
    return [(i * wide, (i + 1) * wide) for i in range(count)]


def cost():
    return pl.CostEstimate(flops=1, bytes_accessed=1, transcendentals=0)


def params():
    return pltpu.CompilerParams(vmem_limit_bytes=10 * 2**20)


def assemble_kernel(count, starts_ref, after_ref, *refs):
    keys_ref = refs[count]
    for i, piece in enumerate(refs[:count]):
        keys_ref[pl.ds(pl.multiple_of(starts_ref[i], 16), piece.shape[0]), :] = piece[...]


def assembled(pieces, starts, keys, after):
    return pl.pallas_call(
        functools.partial(assemble_kernel, len(pieces)),
        in_specs=[SMEM, ANY] + [VMEM] * len(pieces),
        out_specs=VMEM,
        out_shape=jax.ShapeDtypeStruct((keys, pieces[0].shape[1]), pieces[0].dtype),
        compiler_params=params(),
        cost_estimate=cost(),
        name="assemble",
    )(starts, after, *pieces)


def multiply(left, ahead, keys_ref, weights_ref, early, wide_ref, held_ref, arrived):
    wide = wide_ref.shape[1]
    deep = keys_ref.shape[1] // STEPS

    def copy(step):
        return pltpu.make_async_copy(
            weights_ref.at[pl.ds(step * deep, deep), pl.ds(left, wide)],
            held_ref.at[step % SLOTS],
            arrived.at[step % SLOTS],
        )

    for step in range(ahead, min(ahead + SLOTS, STEPS)):
        copy(step).start()
    for step in range(STEPS):
        if step < ahead:
            weights = early[0][step * deep : (step + 1) * deep, :]
        else:
            copy(step).wait()
            weights = held_ref[step % SLOTS]
        part = jnp.dot(
            keys_ref[:, step * deep : (step + 1) * deep],
            weights,
            preferred_element_type=jnp.float32,
        )
        if step >= ahead and step + SLOTS < STEPS:
            copy(step + SLOTS).start()
        wide_ref[...] = part if step == 0 else wide_ref[...] + part


def against(left, at_ref, final_ref, came_ref, stored_ref, before, terms_ref, piece_ref, rows_ref):
    @pl.when(at_ref[0] != 0)
    def _():
        rows_ref[...] = final_ref[...]

    @pl.when(at_ref[0] == 0)
    def _():
        rows_ref[...] = came_ref[...]

    batches, slots, _ = stored_ref.shape
    wide = rows_ref.shape[1]
    term = lax.dot_general(
        rows_ref[...],
        stored_ref[:, :, left : left + wide].reshape(batches * slots, wide),
        (((1,), (1,)), ((), ())),
        preferred_element_type=jnp.float32,
    )
    terms_ref[...] = before[0][...] + term if before else term
    piece_ref[...] = rows_ref[pl.ds(pl.multiple_of(at_ref[1], 16), piece_ref.shape[0]), :]


def work_kernel(product, contract, joined, at_ref, after_ref, *refs):
    refs = list(refs)
    take = lambda n: [refs.pop(0) for _ in range(n)]
    if product:
        factors = take(2)
        early = take(1 if product[1] else 0)
    if contract:
        rows = take(3)
        before = take(contract[1])
        pieces = take(joined)
    if product:
        (wide_ref,) = take(1)
    if contract:
        terms_ref, piece_ref = take(2)
    if joined:
        (whole_ref,) = take(1)
    if product:
        multiply(*product, *factors, early, wide_ref, *take(2))
    if contract:
        against(contract[0], at_ref, *rows, before, terms_ref, piece_ref, *take(1))
    if joined:
        left = 0
        for piece in pieces + [piece_ref]:
            whole_ref[:, left : left + piece.shape[1]] = piece[...]
            left += piece.shape[1]


def work(at, after, product=None, contract=None, pieces=()):
    operands, specs, shapes, scratch = [at, after], [SMEM, ANY], [], []
    product_at = contract_at = None
    if product:
        keys, weights, early, span = product
        depth, rows, wide = weights.shape[0], keys.shape[0], span[1] - span[0]
        product_at = (span[0], AHEAD if early else 0)
        operands += [keys, weights, *early]
        specs += [VMEM, ANY] + [VMEM] * len(early)
        shapes += [jax.ShapeDtypeStruct((rows, wide), jnp.float32)]
        scratch += [
            pltpu.VMEM((SLOTS, depth // STEPS, wide), weights.dtype),
            pltpu.SemaphoreType.DMA((SLOTS,)),
        ]
    if contract:
        final, came, stored, terms, left, block = contract
        rows, wide = final.shape
        before = [] if terms is None else [terms]
        contract_at = (left, len(before))
        operands += [final, came, stored, *before, *pieces]
        specs += [VMEM] * (3 + len(before) + len(pieces))
        shapes += [
            jax.ShapeDtypeStruct((rows, stored.shape[0] * stored.shape[1]), jnp.float32),
            jax.ShapeDtypeStruct((block, wide), jnp.bfloat16),
        ]
        scratch += [pltpu.VMEM((rows, wide), jnp.bfloat16)]
    if pieces:
        columns = sum(p.shape[1] for p in pieces) + wide
        shapes += [jax.ShapeDtypeStruct((block, columns), jnp.bfloat16)]
    return pl.pallas_call(
        functools.partial(work_kernel, product_at, contract_at, len(pieces)),
        in_specs=specs,
        out_specs=[VMEM] * len(shapes),
        out_shape=shapes,
        scratch_shapes=scratch,
        compiler_params=params(),
        cost_estimate=cost(),
        name="work",
    )(*operands)


def tick_kernel(names, outs, at_ref, after_ref, *refs):
    given = dict(zip(names, refs))
    made = dict(zip(outs, refs[len(names) :]))
    if "total" in made:
        total = given["wide"][...] + given["outer"][...].astype(jnp.float32)
        made["total"][...] = total
        made["across"][...] = total.astype(jnp.bfloat16)
    if "final" in made:
        final = (given["held"][...] + given["middle"][...].astype(jnp.float32)).astype(jnp.bfloat16)
        made["final"][...] = final
    if "along" in made:
        along = given["next"][...].astype(jnp.bfloat16)
        if "final" in made:
            along = jnp.where(at_ref[0] != 0, final, along)
        made["along"][...] = along


def tick(at, after, outs, **given):
    shape = next(iter(given.values())).shape
    wide = {"total": jnp.float32}
    made = pl.pallas_call(
        functools.partial(tick_kernel, tuple(given), outs),
        in_specs=[SMEM, ANY] + [VMEM] * len(given),
        out_specs=[VMEM] * len(outs),
        out_shape=[jax.ShapeDtypeStruct(shape, wide.get(name, jnp.bfloat16)) for name in outs],
        compiler_params=params(),
        cost_estimate=cost(),
        name="tick",
    )(at, after, *given.values())
    return dict(zip(outs, made))


def along_line(at, multiplied, contracted, count):
    wide, total, final = {}, {}, {}
    (wide[0],) = multiplied(0, at)
    outer = middle = None
    after = wide[0]
    for k in range(count + 2):
        outs, given = [], {}
        if 1 <= k <= count:
            outs += ["total", "across"]
            given.update(wide=wide[k - 1], outer=outer)
        if k >= 2:
            outs += ["final"]
            given.update(held=total[k - 2], middle=middle)
        if k < count:
            outs += ["along"]
            given.update(next=wide[k])
        made = tick(at, after, tuple(outs), **given)
        earlier = outer
        if k >= 2:
            final[k - 2] = made["final"]
        if 1 <= k <= count:
            total[k - 1] = made["total"]
            middle = lax.ppermute(made["across"], "row", [(1, 2), (2, 1)])
        pairs = ([(0, 1), (3, 2)] if k < count else []) + ([(1, 0), (2, 3)] if k >= 2 else [])
        sent = made["along"] if k < count else made["final"] if k >= 2 else made["across"]
        if pairs:
            outer = lax.ppermute(sent, "row", pairs)
        after = sent
        if k + 1 < count or k >= 3:
            product = k + 1 if k + 1 < count else None
            contract = (k - 3, final[k - 3], earlier) if k >= 3 else None
            out = multiplied(product, after, contract)
            if product is not None:
                wide[product] = out[0]
            after = out[-1]
    contracted(count - 1, final[count - 1], outer, after)


def select_kernel(row_ref, batch_ref, used_ref, length_ref, slot_ref, kept_ref, came_ref, out_ref, held_ref):
    count, batches, rows, slots = held_ref.shape
    half = count // 2
    for i in range(count):
        part = kept_ref[i, 0] if i < half else came_ref[i - half, 0]
        for b in range(batches):
            held_ref[i, b] = part[:, b * slots : (b + 1) * slots]
    row = row_ref[0]
    column = lax.broadcasted_iota(jnp.int32, (rows, slots), 1)
    for place in range(out_ref.shape[1]):
        batch = batch_ref[row, place]
        slot = slot_ref[batch]
        owner = lax.div(slot, batches)
        length = jnp.where(place < used_ref[row], length_ref[batch], 0)
        value = held_ref[owner ^ row, slot - owner * batches]
        out_ref[0, place] = jnp.where(column < length, value, 0.0)


def selected(kept, came, row_index, pair_batch, pair_count, batch_length, batch_slot, batches):
    half, _, rows, wide = kept.shape
    slots = wide // batches
    places = pair_batch.shape[1]
    return pl.pallas_call(
        select_kernel,
        in_specs=[SMEM] * 5 + [VMEM] * 2,
        out_specs=VMEM,
        out_shape=jax.ShapeDtypeStruct((1, places, rows, slots), jnp.float32),
        scratch_shapes=[pltpu.VMEM((2 * half, batches, rows, slots), jnp.float32)],
        cost_estimate=cost(),
        name="select",
    )(row_index[None], pair_batch, pair_count, batch_length, batch_slot, kept, came)


def shards(new_keys, precision, stored_keys, pair_batch, pair_count, batch_length, batch_slot):
    row_count = lax.axis_size("row")
    col_count = lax.axis_size("col")
    row_index = lax.axis_index("row")
    col_index = lax.axis_index("col")
    total_keys = new_keys.shape[0] * col_count
    block = total_keys // row_count
    batches = stored_keys.shape[0]
    half = row_count // 2

    away = jnp.where(row_index < half, half - 1 - row_index, row_index - half)
    at = jnp.stack([(away == 0).astype(jnp.int32), row_index * block])
    spans = ranges(precision.shape[1])
    count = len(spans)
    early = []

    def fetch(after):
        held, token = fetched(precision, spans[0], after)
        early.append(held)
        return token

    pieces, starts, token = gathered(new_keys, col_count, col_index, fetch)
    order = list(range(1, len(pieces))) + [0]
    keys = assembled([pieces[i] for i in order], jnp.stack([starts[i] for i in order]), total_keys, token)
    terms = None
    whitened = []

    def multiplied(part, after, contract=None):
        nonlocal terms
        product = None
        if part is not None:
            product = (keys, precision, [] if part else early, spans[part])
        if contract is not None:
            number, final, came = contract
            contract = (final, came, stored_keys, terms, spans[number][0], block)
        joined = whitened if contract is not None and number == count - 1 else []
        out = work(at, after, product, contract, joined)
        if contract is not None:
            first = 1 if product else 0
            terms = out[first]
            whitened.append(out[-1])
        return out

    def contracted(part, final, came, after):
        multiplied(None, after, (part, final, came))

    if row_count == 4:
        along_line(at, multiplied, contracted, count)
    else:
        after = at
        for part in range(count):
            (wide,) = multiplied(part, after)
            every = lax.psum(wide, "row").astype(jnp.bfloat16)
            contracted(part, every, every, wide)
            after = whitened[-1]

    share = block // col_count
    sums = terms.reshape(row_count, col_count, share, terms.shape[1])
    bit = 1
    while bit < col_count:
        if col_count == 8 and bit == 2:
            other = [lax.dynamic_index_in_dim(sums, (col_index // 2) ^ f, 1, keepdims=False) for f in range(4)]
            sums = other[0] + sum(flipped(other[f], 2 * f, col_count) for f in (3, 2, 1))
            sums = sums[:, None]
            break
        pairs = sums.reshape(row_count, sums.shape[1] // 2, 2, share, sums.shape[3])
        mine = (col_index // bit) % 2
        kept = lax.dynamic_index_in_dim(pairs, mine, 2, keepdims=False)
        left = lax.dynamic_index_in_dim(pairs, 1 - mine, 2, keepdims=False)
        sums = kept + flipped(left, bit, col_count)
        bit *= 2
    parts = [sums[None, :, 0]]
    bit = 1
    while bit < row_count:
        sums = jnp.concatenate(parts)
        pairs = sums.reshape(bit, sums.shape[1] // 2, 2, share, sums.shape[3])
        mine = (row_index // bit) % 2
        kept = lax.dynamic_index_in_dim(pairs, mine, 2, keepdims=False)
        left = lax.dynamic_index_in_dim(pairs, 1 - mine, 2, keepdims=False)
        parts = [kept, lax.ppermute(left, "row", [(r, r ^ bit) for r in range(row_count)])]
        bit *= 2
    shares = selected(*parts, row_index, pair_batch, pair_count, batch_length, batch_slot, batches)
    return (whitened[-1], shares)


def solution(mesh):
    placed = (P("col", "row"), P("row", "col"), P("row", None, "col"), P(), P(), P(), P())
    return jax.shard_map(
        shards,
        mesh=mesh,
        in_specs=placed,
        out_specs=(P("row", "col"), P("row", None, "col", None)),
        check_vma=False,
    )
```

```python
import functools

import jax
import jax.numpy as jnp
from jax import lax
from jax.experimental import pallas as pl
from jax.experimental.pallas import tpu as pltpu
from jax.sharding import PartitionSpec as P

PARTS = 4
STEPS = 7
SLOTS = 4
LANES = 128
VMEM = pl.BlockSpec(memory_space=pltpu.VMEM)
ANY = pl.BlockSpec(memory_space=pl.ANY)
SMEM = pl.BlockSpec(memory_space=pltpu.SMEM)


def flipped(array, bit, count):
    return lax.ppermute(array, "col", [(c, c ^ bit) for c in range(count)])


def gathered(new_keys, col_count, col_index):
    rows = new_keys.shape[0]
    if col_count != 8:
        start = col_index * rows
        return [new_keys, lax.all_gather(new_keys, "col", axis=0, tiled=True)], [start, jnp.int32(0)]
    half = rows // 2
    by_x = flipped(new_keys, 2, 8)
    by_y = flipped(new_keys, 4, 8)
    by_core = flipped(new_keys, 1, 8)
    own, low, high = halved(new_keys, by_x, by_y)
    low = flipped(low, 4, 8)
    high = flipped(high, 2, 8)
    x_core = flipped(by_x, 1, 8)
    y_core = flipped(by_y, 1, 8)
    low_core = flipped(low, 1, 8)
    high_core = flipped(high, 1, 8)
    pieces = [own, by_core, by_x, x_core, by_y, y_core, low, high, low_core, high_core]
    of = [0, 1, 2, 3, 4, 5, 6, 6, 7, 7]
    within = [0] * 7 + [half, 0, half]
    return pieces, [(col_index ^ f) * rows + w for f, w in zip(of, within)]


def halved_kernel(own_ref, x_ref, y_ref, keys_ref, low_ref, high_ref):
    keys_ref[...] = own_ref[...]
    half = low_ref.shape[0]
    low_ref[...] = x_ref[:half]
    high_ref[...] = y_ref[half:]


def halved(own, by_x, by_y):
    rows, depth = by_x.shape
    return pl.pallas_call(
        halved_kernel,
        in_specs=[VMEM] * 3,
        out_specs=[VMEM] * 3,
        out_shape=[
            jax.ShapeDtypeStruct((rows, depth), own.dtype),
            *[jax.ShapeDtypeStruct((rows // 2, depth), by_x.dtype)] * 2,
        ],
        compiler_params=params(),
        cost_estimate=cost(),
        name="halved",
    )(own, by_x, by_y)


def ranges(columns):
    tiles = columns // LANES
    count = max(n for n in range(1, PARTS + 1) if tiles % n == 0)
    wide = tiles // count * LANES
    return [(i * wide, (i + 1) * wide) for i in range(count)]


def cost():
    return pl.CostEstimate(flops=1, bytes_accessed=1, transcendentals=0)


def params():
    return pltpu.CompilerParams(vmem_limit_bytes=18 * 2**20)


def assemble_kernel(count, starts_ref, *refs):
    keys_ref = refs[count]
    for i, piece in enumerate(refs[:count]):
        keys_ref[pl.ds(pl.multiple_of(starts_ref[i], 16), piece.shape[0]), :] = piece[...]


def assembled(pieces, starts, keys):
    return pl.pallas_call(
        functools.partial(assemble_kernel, len(pieces)),
        in_specs=[SMEM] + [VMEM] * len(pieces),
        out_specs=VMEM,
        out_shape=jax.ShapeDtypeStruct((keys, pieces[0].shape[1]), pieces[0].dtype),
        compiler_params=params(),
        cost_estimate=cost(),
        name="assemble",
    )(starts, *pieces)


def multiply(left, keys_ref, weights_ref, wide_ref, sent, held_ref, arrived):
    wide = wide_ref.shape[1]
    deep = keys_ref.shape[1] // STEPS
    slots = held_ref.shape[0]

    def copy(step):
        return pltpu.make_async_copy(
            weights_ref.at[pl.ds(step * deep, deep), pl.ds(left, wide)],
            held_ref.at[step % slots],
            arrived.at[step % slots],
        )

    for step in range(slots):
        copy(step).start()
    for step in range(STEPS):
        copy(step).wait()
        part = jnp.dot(
            keys_ref[:, step * deep : (step + 1) * deep],
            held_ref[step % slots],
            preferred_element_type=jnp.float32,
        )
        if step + slots < STEPS:
            copy(step + slots).start()
        total = part if step == 0 else wide_ref[...] + part
        wide_ref[...] = total
        if sent and step == STEPS - 1:
            sent[0][...] = total.astype(sent[0].dtype)


def against(left, at_ref, final_ref, came_ref, stored_ref, before, terms_ref, piece_ref, rows_ref):
    @pl.when(at_ref[0] != 0)
    def _():
        rows_ref[...] = final_ref[...]

    @pl.when(at_ref[0] == 0)
    def _():
        rows_ref[...] = came_ref[...]

    batches, slots, _ = stored_ref.shape
    wide = rows_ref.shape[1]
    term = lax.dot_general(
        rows_ref[...],
        stored_ref[:, :, left : left + wide].reshape(batches * slots, wide),
        (((1,), (1,)), ((), ())),
        preferred_element_type=jnp.float32,
    )
    terms_ref[...] = before[0][...] + term if before else term
    piece_ref[...] = rows_ref[pl.ds(pl.multiple_of(at_ref[1], 16), piece_ref.shape[0]), :]


def work_kernel(product, contract, joined, at_ref, after_ref, *refs):
    refs = list(refs)
    take = lambda n: [refs.pop(0) for _ in range(n)]
    if product:
        factors = take(2)
    if contract:
        rows = take(3)
        before = take(contract[1])
        pieces = take(joined)
    if product:
        (wide_ref,) = take(1)
        sent = take(1 if product[1] else 0)
    if contract:
        terms_ref, piece_ref = take(2)
    if joined:
        (whole_ref,) = take(1)
    if product:
        multiply(product[0], *factors, wide_ref, sent, *take(2))
    if contract:
        against(contract[0], at_ref, *rows, before, terms_ref, piece_ref, *take(1))
    if joined:
        left = 0
        for piece in pieces + [piece_ref]:
            whole_ref[:, left : left + piece.shape[1]] = piece[...]
            left += piece.shape[1]


def work(at, after, product=None, contract=None, pieces=()):
    operands, specs, shapes, scratch = [at, after], [SMEM, ANY], [], []
    product_at = contract_at = None
    if product:
        keys, weights, span, first = product
        depth, rows, wide = weights.shape[0], keys.shape[0], span[1] - span[0]
        product_at = (span[0], first)
        operands += [keys, weights]
        specs += [VMEM, ANY]
        shapes += [jax.ShapeDtypeStruct((rows, wide), jnp.float32)]
        shapes += [jax.ShapeDtypeStruct((rows, wide), jnp.bfloat16)] * first
        slots = STEPS if first else SLOTS
        scratch += [
            pltpu.VMEM((slots, depth // STEPS, wide), weights.dtype),
            pltpu.SemaphoreType.DMA((slots,)),
        ]
    if contract:
        final, came, stored, terms, left, block = contract
        rows, wide = final.shape
        before = [] if terms is None else [terms]
        contract_at = (left, len(before))
        operands += [final, came, stored, *before, *pieces]
        specs += [VMEM] * (3 + len(before) + len(pieces))
        shapes += [
            jax.ShapeDtypeStruct((rows, stored.shape[0] * stored.shape[1]), jnp.float32),
            jax.ShapeDtypeStruct((block, wide), jnp.bfloat16),
        ]
        scratch += [pltpu.VMEM((rows, wide), jnp.bfloat16)]
    if pieces:
        columns = sum(p.shape[1] for p in pieces) + wide
        shapes += [jax.ShapeDtypeStruct((block, columns), jnp.bfloat16)]
    return pl.pallas_call(
        functools.partial(work_kernel, product_at, contract_at, len(pieces)),
        in_specs=specs,
        out_specs=[VMEM] * len(shapes),
        out_shape=shapes,
        scratch_shapes=scratch,
        compiler_params=params(),
        cost_estimate=cost(),
        name="work",
    )(*operands)


def tick_kernel(names, outs, at_ref, after_ref, *refs):
    given = dict(zip(names, refs))
    made = dict(zip(outs, refs[len(names) :]))
    if "total" in made:
        total = given["wide"][...] + given["outer"][...].astype(jnp.float32)
        made["total"][...] = total
        made["across"][...] = total.astype(jnp.bfloat16)
    if "final" in made:
        final = (given["held"][...] + given["middle"][...].astype(jnp.float32)).astype(jnp.bfloat16)
        made["final"][...] = final
    if "along" in made:
        along = given["next"][...].astype(jnp.bfloat16)
        if "final" in made:
            along = jnp.where(at_ref[0] != 0, final, along)
        made["along"][...] = along


def tick(at, after, outs, **given):
    shape = next(iter(given.values())).shape
    wide = {"total": jnp.float32}
    made = pl.pallas_call(
        functools.partial(tick_kernel, tuple(given), outs),
        in_specs=[SMEM, ANY] + [VMEM] * len(given),
        out_specs=[VMEM] * len(outs),
        out_shape=[jax.ShapeDtypeStruct(shape, wide.get(name, jnp.bfloat16)) for name in outs],
        compiler_params=params(),
        cost_estimate=cost(),
        name="tick",
    )(at, after, *given.values())
    return dict(zip(outs, made))


def along_line(at, multiplied, contracted, count):
    wide, total, final = {}, {}, {}
    wide[0], sent = multiplied(0, at)
    outer = lax.ppermute(sent, "row", [(0, 1), (3, 2)])
    middle, after = None, sent
    if count > 1:
        (wide[1],) = multiplied(1, after)
        after = wide[1]
    for k in range(1, count + 2):
        outs, given = [], {}
        if 1 <= k <= count:
            outs += ["total", "across"]
            given.update(wide=wide[k - 1], outer=outer)
        if k >= 2:
            outs += ["final"]
            given.update(held=total[k - 2], middle=middle)
        if k < count:
            outs += ["along"]
            given.update(next=wide[k])
        made = tick(at, after, tuple(outs), **given)
        earlier = outer
        if k >= 2:
            final[k - 2] = made["final"]
        if 1 <= k <= count:
            total[k - 1] = made["total"]
            middle = lax.ppermute(made["across"], "row", [(1, 2), (2, 1)])
        pairs = ([(0, 1), (3, 2)] if k < count else []) + ([(1, 0), (2, 3)] if k >= 2 else [])
        sent = made["along"] if k < count else made["final"] if k >= 2 else made["across"]
        if pairs:
            outer = lax.ppermute(sent, "row", pairs)
        after = sent
        if k + 1 < count or k >= 3:
            product = k + 1 if k + 1 < count else None
            contract = (k - 3, final[k - 3], earlier) if k >= 3 else None
            out = multiplied(product, after, contract)
            if product is not None:
                wide[product] = out[0]
            after = out[-1]
    contracted(count - 1, final[count - 1], outer, after)


def select_kernel(row_ref, batch_ref, used_ref, length_ref, slot_ref, sums_ref, out_ref, held_ref):
    count, batches, rows, slots = held_ref.shape
    for i in range(count):
        for b in range(batches):
            held_ref[i, b] = sums_ref[i, :, b * slots : (b + 1) * slots]
    row = row_ref[0]
    column = lax.broadcasted_iota(jnp.int32, (rows, slots), 1)
    for place in range(out_ref.shape[1]):
        batch = batch_ref[row, place]
        slot = slot_ref[batch]
        owner = lax.div(slot, batches)
        length = jnp.where(place < used_ref[row], length_ref[batch], 0)
        value = held_ref[owner, slot - owner * batches]
        out_ref[0, place] = jnp.where(column < length, value, 0.0)


def selected(sums, row_index, pair_batch, pair_count, batch_length, batch_slot, batches):
    count, rows, wide = sums.shape
    slots = wide // batches
    places = pair_batch.shape[1]
    return pl.pallas_call(
        select_kernel,
        in_specs=[SMEM] * 5 + [VMEM],
        out_specs=VMEM,
        out_shape=jax.ShapeDtypeStruct((1, places, rows, slots), jnp.float32),
        scratch_shapes=[pltpu.VMEM((count, batches, rows, slots), jnp.float32)],
        cost_estimate=cost(),
        name="select",
    )(row_index[None], pair_batch, pair_count, batch_length, batch_slot, sums)


def shards(new_keys, precision, stored_keys, pair_batch, pair_count, batch_length, batch_slot):
    row_count = lax.axis_size("row")
    col_count = lax.axis_size("col")
    row_index = lax.axis_index("row")
    col_index = lax.axis_index("col")
    total_keys = new_keys.shape[0] * col_count
    block = total_keys // row_count
    batches = stored_keys.shape[0]
    half = row_count // 2

    away = jnp.where(row_index < half, half - 1 - row_index, row_index - half)
    at = jnp.stack([(away == 0).astype(jnp.int32), row_index * block])
    spans = ranges(precision.shape[1])
    count = len(spans)

    pieces, starts = gathered(new_keys, col_count, col_index)
    order = list(range(1, len(pieces))) + [0]
    keys = assembled([pieces[i] for i in order], jnp.stack([starts[i] for i in order]), total_keys)
    terms = None
    whitened = []

    def multiplied(part, after, contract=None):
        nonlocal terms
        product = None
        if part is not None:
            product = (keys, precision, spans[part], part == 0)
        if contract is not None:
            number, final, came = contract
            contract = (final, came, stored_keys, terms, spans[number][0], block)
        joined = whitened if contract is not None and number == count - 1 else []
        out = work(at, after, product, contract, joined)
        if contract is not None:
            terms = out[1 if product else 0]
            whitened.append(out[-1])
        return out

    def contracted(part, final, came, after):
        multiplied(None, after, (part, final, came))

    if row_count == 4:
        along_line(at, multiplied, contracted, count)
    else:
        after = at
        for part in range(count):
            wide = multiplied(part, after)[0]
            every = lax.psum(wide, "row").astype(jnp.bfloat16)
            contracted(part, every, every, wide)
            after = whitened[-1]

    share = block // col_count
    sums = terms.reshape(row_count, col_count, share, terms.shape[1])
    bit = 1
    while bit < col_count:
        if col_count == 8 and bit == 2:
            other = [lax.dynamic_index_in_dim(sums, (col_index // 2) ^ f, 1, keepdims=False) for f in range(4)]
            sums = other[0] + sum(flipped(other[f], 2 * f, col_count) for f in (3, 2, 1))
            sums = sums[:, None]
            break
        pairs = sums.reshape(row_count, sums.shape[1] // 2, 2, share, sums.shape[3])
        mine = (col_index // bit) % 2
        kept = lax.dynamic_index_in_dim(pairs, mine, 2, keepdims=False)
        left = lax.dynamic_index_in_dim(pairs, 1 - mine, 2, keepdims=False)
        sums = kept + flipped(left, bit, col_count)
        bit *= 2
    sums = lax.all_to_all(sums[:, 0], "row", split_axis=0, concat_axis=0, tiled=True)
    shares = selected(sums, row_index, pair_batch, pair_count, batch_length, batch_slot, batches)
    return (whitened[-1], shares)


def solution(mesh):
    placed = (P("col", "row"), P("row", "col"), P("row", None, "col"), P(), P(), P(), P())
    return jax.shard_map(
        shards,
        mesh=mesh,
        in_specs=placed,
        out_specs=(P("row", "col"), P("row", None, "col", None)),
        check_vma=False,
    )
```

```python
import functools

import jax
import jax.numpy as jnp
from jax import lax
from jax.experimental import pallas as pl
from jax.experimental.pallas import tpu as pltpu
from jax.sharding import PartitionSpec as P

PARTS = 4
STEPS = 7
SLOTS = 4
LANES = 128
VMEM = pl.BlockSpec(memory_space=pltpu.VMEM)
ANY = pl.BlockSpec(memory_space=pl.ANY)
SMEM = pl.BlockSpec(memory_space=pltpu.SMEM)


def flipped(array, bit, count):
    return lax.ppermute(array, "col", [(c, c ^ bit) for c in range(count)])


def gathered(new_keys, col_count, col_index):
    rows = new_keys.shape[0]
    if col_count != 8:
        start = col_index * rows
        return [new_keys, lax.all_gather(new_keys, "col", axis=0, tiled=True)], [start, jnp.int32(0)]
    pieces = {0: new_keys}
    for far in (2, 4, 6):
        pieces[far] = flipped(new_keys, far, 8)
    for far in (0, 2, 4, 6):
        pieces[far + 1] = flipped(pieces[far], 1, 8)
    order = sorted(pieces)
    return [pieces[f] for f in order], [(col_index ^ f) * rows for f in order]


def ranges(columns):
    tiles = columns // LANES
    count = max(n for n in range(1, PARTS + 1) if tiles % n == 0)
    wide = tiles // count * LANES
    return [(i * wide, (i + 1) * wide) for i in range(count)]


def cost():
    return pl.CostEstimate(flops=1, bytes_accessed=1, transcendentals=0)


def params():
    return pltpu.CompilerParams(vmem_limit_bytes=18 * 2**20)


def assemble_kernel(count, starts_ref, own_ref, *refs):
    keys_ref, held_ref, arrived = refs[count:]
    copy = pltpu.make_async_copy(own_ref, held_ref, arrived)
    copy.start()
    for i, piece in enumerate(refs[:count]):
        keys_ref[pl.ds(pl.multiple_of(starts_ref[i + 1], 16), piece.shape[0]), :] = piece[...]
    copy.wait()
    keys_ref[pl.ds(pl.multiple_of(starts_ref[0], 16), own_ref.shape[0]), :] = held_ref[...]


def assembled(pieces, starts, keys):
    own = pieces[0]
    return pl.pallas_call(
        functools.partial(assemble_kernel, len(pieces) - 1),
        in_specs=[SMEM, ANY] + [VMEM] * (len(pieces) - 1),
        out_specs=VMEM,
        out_shape=jax.ShapeDtypeStruct((keys, own.shape[1]), own.dtype),
        scratch_shapes=[pltpu.VMEM(own.shape, own.dtype), pltpu.SemaphoreType.DMA],
        compiler_params=params(),
        cost_estimate=cost(),
        name="assemble",
    )(starts, *pieces)


def multiply(left, keys_ref, weights_ref, wide_ref, sent, held_ref, arrived):
    wide = wide_ref.shape[1]
    deep = keys_ref.shape[1] // STEPS
    slots = held_ref.shape[0]

    def copy(step):
        return pltpu.make_async_copy(
            weights_ref.at[pl.ds(step * deep, deep), pl.ds(left, wide)],
            held_ref.at[step % slots],
            arrived.at[step % slots],
        )

    for step in range(slots):
        copy(step).start()
    for step in range(STEPS):
        copy(step).wait()
        part = jnp.dot(
            keys_ref[:, step * deep : (step + 1) * deep],
            held_ref[step % slots],
            preferred_element_type=jnp.float32,
        )
        if step + slots < STEPS:
            copy(step + slots).start()
        total = part if step == 0 else wide_ref[...] + part
        wide_ref[...] = total
        if sent and step == STEPS - 1:
            sent[0][...] = total.astype(sent[0].dtype)


def against(left, at_ref, final_ref, came_ref, stored_ref, before, terms_ref, piece_ref, rows_ref):
    @pl.when(at_ref[0] != 0)
    def _():
        rows_ref[...] = final_ref[...]

    @pl.when(at_ref[0] == 0)
    def _():
        rows_ref[...] = came_ref[...]

    batches, slots, _ = stored_ref.shape
    wide = rows_ref.shape[1]
    term = lax.dot_general(
        rows_ref[...],
        stored_ref[:, :, left : left + wide].reshape(batches * slots, wide),
        (((1,), (1,)), ((), ())),
        preferred_element_type=jnp.float32,
    )
    terms_ref[...] = before[0][...] + term if before else term
    piece_ref[...] = rows_ref[pl.ds(pl.multiple_of(at_ref[1], 16), piece_ref.shape[0]), :]


def work_kernel(product, contract, joined, at_ref, after_ref, *refs):
    refs = list(refs)
    take = lambda n: [refs.pop(0) for _ in range(n)]
    if product:
        factors = take(2)
    if contract:
        rows = take(3)
        before = take(contract[1])
        pieces = take(joined)
    if product:
        (wide_ref,) = take(1)
        sent = take(1 if product[1] else 0)
    if contract:
        terms_ref, piece_ref = take(2)
    if joined:
        (whole_ref,) = take(1)
    if product:
        multiply(product[0], *factors, wide_ref, sent, *take(2))
    if contract:
        against(contract[0], at_ref, *rows, before, terms_ref, piece_ref, *take(1))
    if joined:
        left = 0
        for piece in pieces + [piece_ref]:
            whole_ref[:, left : left + piece.shape[1]] = piece[...]
            left += piece.shape[1]


def work(at, after, product=None, contract=None, pieces=()):
    operands, specs, shapes, scratch = [at, after], [SMEM, ANY], [], []
    product_at = contract_at = None
    if product:
        keys, weights, span, first = product
        depth, rows, wide = weights.shape[0], keys.shape[0], span[1] - span[0]
        product_at = (span[0], first)
        operands += [keys, weights]
        specs += [VMEM, ANY]
        shapes += [jax.ShapeDtypeStruct((rows, wide), jnp.float32)]
        shapes += [jax.ShapeDtypeStruct((rows, wide), jnp.bfloat16)] * first
        slots = STEPS if first else SLOTS
        scratch += [
            pltpu.VMEM((slots, depth // STEPS, wide), weights.dtype),
            pltpu.SemaphoreType.DMA((slots,)),
        ]
    if contract:
        final, came, stored, terms, left, block = contract
        rows, wide = final.shape
        before = [] if terms is None else [terms]
        contract_at = (left, len(before))
        operands += [final, came, stored, *before, *pieces]
        specs += [VMEM] * (3 + len(before) + len(pieces))
        shapes += [
            jax.ShapeDtypeStruct((rows, stored.shape[0] * stored.shape[1]), jnp.float32),
            jax.ShapeDtypeStruct((block, wide), jnp.bfloat16),
        ]
        scratch += [pltpu.VMEM((rows, wide), jnp.bfloat16)]
    if pieces:
        columns = sum(p.shape[1] for p in pieces) + wide
        shapes += [jax.ShapeDtypeStruct((block, columns), jnp.bfloat16)]
    return pl.pallas_call(
        functools.partial(work_kernel, product_at, contract_at, len(pieces)),
        in_specs=specs,
        out_specs=[VMEM] * len(shapes),
        out_shape=shapes,
        scratch_shapes=scratch,
        compiler_params=params(),
        cost_estimate=cost(),
        name="work",
    )(*operands)


def tick_kernel(names, outs, at_ref, after_ref, *refs):
    given = dict(zip(names, refs))
    made = dict(zip(outs, refs[len(names) :]))
    if "total" in made:
        total = given["wide"][...] + given["outer"][...].astype(jnp.float32)
        made["total"][...] = total
        made["across"][...] = total.astype(jnp.bfloat16)
    if "final" in made:
        final = (given["held"][...] + given["middle"][...].astype(jnp.float32)).astype(jnp.bfloat16)
        made["final"][...] = final
    if "along" in made:
        along = given["next"][...].astype(jnp.bfloat16)
        if "final" in made:
            along = jnp.where(at_ref[0] != 0, final, along)
        made["along"][...] = along


def tick(at, after, outs, **given):
    shape = next(iter(given.values())).shape
    wide = {"total": jnp.float32}
    made = pl.pallas_call(
        functools.partial(tick_kernel, tuple(given), outs),
        in_specs=[SMEM, ANY] + [VMEM] * len(given),
        out_specs=[VMEM] * len(outs),
        out_shape=[jax.ShapeDtypeStruct(shape, wide.get(name, jnp.bfloat16)) for name in outs],
        compiler_params=params(),
        cost_estimate=cost(),
        name="tick",
    )(at, after, *given.values())
    return dict(zip(outs, made))


def along_line(at, multiplied, contracted, count):
    wide, total, final = {}, {}, {}
    wide[0], sent = multiplied(0, at)
    outer = lax.ppermute(sent, "row", [(0, 1), (3, 2)])
    middle, after = None, sent
    if count > 1:
        (wide[1],) = multiplied(1, after)
        after = wide[1]
    for k in range(1, count + 2):
        outs, given = [], {}
        if 1 <= k <= count:
            outs += ["total", "across"]
            given.update(wide=wide[k - 1], outer=outer)
        if k >= 2:
            outs += ["final"]
            given.update(held=total[k - 2], middle=middle)
        if k < count:
            outs += ["along"]
            given.update(next=wide[k])
        made = tick(at, after, tuple(outs), **given)
        earlier = outer
        if k >= 2:
            final[k - 2] = made["final"]
        if 1 <= k <= count:
            total[k - 1] = made["total"]
            middle = lax.ppermute(made["across"], "row", [(1, 2), (2, 1)])
        pairs = ([(0, 1), (3, 2)] if k < count else []) + ([(1, 0), (2, 3)] if k >= 2 else [])
        sent = made["along"] if k < count else made["final"] if k >= 2 else made["across"]
        if pairs:
            outer = lax.ppermute(sent, "row", pairs)
        after = sent
        if k + 1 < count or k >= 3:
            product = k + 1 if k + 1 < count else None
            contract = (k - 3, final[k - 3], earlier) if k >= 3 else None
            out = multiplied(product, after, contract)
            if product is not None:
                wide[product] = out[0]
            after = out[-1]
    contracted(count - 1, final[count - 1], outer, after)


def select_kernel(row_ref, batch_ref, used_ref, length_ref, slot_ref, sums_ref, out_ref, held_ref):
    count, batches, rows, slots = held_ref.shape
    for i in range(count):
        for b in range(batches):
            held_ref[i, b] = sums_ref[i, :, b * slots : (b + 1) * slots]
    row = row_ref[0]
    column = lax.broadcasted_iota(jnp.int32, (rows, slots), 1)
    for place in range(out_ref.shape[1]):
        batch = batch_ref[row, place]
        slot = slot_ref[batch]
        owner = lax.div(slot, batches)
        length = jnp.where(place < used_ref[row], length_ref[batch], 0)
        value = held_ref[owner, slot - owner * batches]
        out_ref[0, place] = jnp.where(column < length, value, 0.0)


def selected(sums, row_index, pair_batch, pair_count, batch_length, batch_slot, batches):
    count, rows, wide = sums.shape
    slots = wide // batches
    places = pair_batch.shape[1]
    return pl.pallas_call(
        select_kernel,
        in_specs=[SMEM] * 5 + [VMEM],
        out_specs=VMEM,
        out_shape=jax.ShapeDtypeStruct((1, places, rows, slots), jnp.float32),
        scratch_shapes=[pltpu.VMEM((count, batches, rows, slots), jnp.float32)],
        cost_estimate=cost(),
        name="select",
    )(row_index[None], pair_batch, pair_count, batch_length, batch_slot, sums)


def shards(new_keys, precision, stored_keys, pair_batch, pair_count, batch_length, batch_slot):
    row_count = lax.axis_size("row")
    col_count = lax.axis_size("col")
    row_index = lax.axis_index("row")
    col_index = lax.axis_index("col")
    total_keys = new_keys.shape[0] * col_count
    block = total_keys // row_count
    batches = stored_keys.shape[0]
    half = row_count // 2

    away = jnp.where(row_index < half, half - 1 - row_index, row_index - half)
    at = jnp.stack([(away == 0).astype(jnp.int32), row_index * block])
    spans = ranges(precision.shape[1])
    count = len(spans)

    pieces, starts = gathered(new_keys, col_count, col_index)
    keys = assembled(pieces, jnp.stack(starts), total_keys)
    terms = None
    whitened = []

    def multiplied(part, after, contract=None):
        nonlocal terms
        product = None
        if part is not None:
            product = (keys, precision, spans[part], part == 0)
        if contract is not None:
            number, final, came = contract
            contract = (final, came, stored_keys, terms, spans[number][0], block)
        joined = whitened if contract is not None and number == count - 1 else []
        out = work(at, after, product, contract, joined)
        if contract is not None:
            terms = out[1 if product else 0]
            whitened.append(out[-1])
        return out

    def contracted(part, final, came, after):
        multiplied(None, after, (part, final, came))

    if row_count == 4:
        along_line(at, multiplied, contracted, count)
    else:
        after = at
        for part in range(count):
            wide = multiplied(part, after)[0]
            every = lax.psum(wide, "row").astype(jnp.bfloat16)
            contracted(part, every, every, wide)
            after = whitened[-1]

    share = block // col_count
    sums = terms.reshape(row_count, col_count, share, terms.shape[1])
    bit = 1
    while bit < col_count:
        if col_count == 8 and bit == 2:
            other = [lax.dynamic_index_in_dim(sums, (col_index // 2) ^ f, 1, keepdims=False) for f in range(4)]
            sums = other[0] + sum(flipped(other[f], 2 * f, col_count) for f in (3, 2, 1))
            sums = sums[:, None]
            break
        pairs = sums.reshape(row_count, sums.shape[1] // 2, 2, share, sums.shape[3])
        mine = (col_index // bit) % 2
        kept = lax.dynamic_index_in_dim(pairs, mine, 2, keepdims=False)
        left = lax.dynamic_index_in_dim(pairs, 1 - mine, 2, keepdims=False)
        sums = kept + flipped(left, bit, col_count)
        bit *= 2
    sums = lax.all_to_all(sums[:, 0], "row", split_axis=0, concat_axis=0, tiled=True)
    shares = selected(sums, row_index, pair_batch, pair_count, batch_length, batch_slot, batches)
    return (whitened[-1], shares)


def solution(mesh):
    placed = (P("col", "row"), P("row", "col"), P("row", None, "col"), P(), P(), P(), P())
    return jax.shard_map(
        shards,
        mesh=mesh,
        in_specs=placed,
        out_specs=(P("row", "col"), P("row", None, "col", None)),
        check_vma=False,
    )
```

```python
import functools

import jax
import jax.numpy as jnp
from jax import lax
from jax.experimental import pallas as pl
from jax.experimental.pallas import tpu as pltpu
from jax.sharding import PartitionSpec as P

PARTS = 4
STEPS = 7
SLOTS = 4
LANES = 128
VMEM = pl.BlockSpec(memory_space=pltpu.VMEM)
ANY = pl.BlockSpec(memory_space=pl.ANY)
SMEM = pl.BlockSpec(memory_space=pltpu.SMEM)


def flipped(array, bit, count):
    return lax.ppermute(array, "col", [(c, c ^ bit) for c in range(count)])


def gathered(new_keys, col_count, col_index):
    rows = new_keys.shape[0]
    if col_count != 8:
        start = col_index * rows
        return [new_keys, lax.all_gather(new_keys, "col", axis=0, tiled=True)], [start, jnp.int32(0)]
    half = rows // 2
    by_x = flipped(new_keys, 2, 8)
    by_y = flipped(new_keys, 4, 8)
    by_core = flipped(new_keys, 1, 8)
    own, low, high = halved(new_keys, by_x, by_y)
    low = flipped(low, 4, 8)
    high = flipped(high, 2, 8)
    x_core = flipped(by_x, 1, 8)
    y_core = flipped(by_y, 1, 8)
    low_core = flipped(low, 1, 8)
    high_core = flipped(high, 1, 8)
    pieces = [own, by_core, by_x, x_core, by_y, y_core, low, high, low_core, high_core]
    of = [0, 1, 2, 3, 4, 5, 6, 6, 7, 7]
    within = [0] * 7 + [half, 0, half]
    return pieces, [(col_index ^ f) * rows + w for f, w in zip(of, within)]


def halved_kernel(own_ref, x_ref, y_ref, keys_ref, low_ref, high_ref):
    keys_ref[...] = own_ref[...]
    half = low_ref.shape[0]
    low_ref[...] = x_ref[:half]
    high_ref[...] = y_ref[half:]


def halved(own, by_x, by_y):
    rows, depth = by_x.shape
    return pl.pallas_call(
        halved_kernel,
        in_specs=[VMEM] * 3,
        out_specs=[VMEM] * 3,
        out_shape=[
            jax.ShapeDtypeStruct((rows, depth), own.dtype),
            *[jax.ShapeDtypeStruct((rows // 2, depth), by_x.dtype)] * 2,
        ],
        compiler_params=params(),
        cost_estimate=cost(),
        name="halved",
    )(own, by_x, by_y)


def ranges(columns):
    tiles = columns // LANES
    count = max(n for n in range(1, PARTS + 1) if tiles % n == 0)
    wide = tiles // count * LANES
    return [(i * wide, (i + 1) * wide) for i in range(count)]


def cost():
    return pl.CostEstimate(flops=1, bytes_accessed=1, transcendentals=0)


def params():
    return pltpu.CompilerParams(vmem_limit_bytes=18 * 2**20)


def assemble_kernel(count, starts_ref, *refs):
    keys_ref = refs[count]
    for i, piece in enumerate(refs[:count]):
        keys_ref[pl.ds(pl.multiple_of(starts_ref[i], 16), piece.shape[0]), :] = piece[...]


def assembled(pieces, starts, keys):
    return pl.pallas_call(
        functools.partial(assemble_kernel, len(pieces)),
        in_specs=[SMEM] + [VMEM] * len(pieces),
        out_specs=VMEM,
        out_shape=jax.ShapeDtypeStruct((keys, pieces[0].shape[1]), pieces[0].dtype),
        compiler_params=params(),
        cost_estimate=cost(),
        name="assemble",
    )(starts, *pieces)


def multiply(left, keys_ref, weights_ref, wide_ref, sent, held_ref, arrived):
    wide = wide_ref.shape[1]
    deep = keys_ref.shape[1] // STEPS
    slots = held_ref.shape[0]

    def copy(step):
        return pltpu.make_async_copy(
            weights_ref.at[pl.ds(step * deep, deep), pl.ds(left, wide)],
            held_ref.at[step % slots],
            arrived.at[step % slots],
        )

    for step in range(slots):
        copy(step).start()
    for step in range(STEPS):
        copy(step).wait()
        part = jnp.dot(
            keys_ref[:, step * deep : (step + 1) * deep],
            held_ref[step % slots],
            preferred_element_type=jnp.float32,
        )
        if step + slots < STEPS:
            copy(step + slots).start()
        total = part if step == 0 else wide_ref[...] + part
        wide_ref[...] = total
        if sent and step == STEPS - 1:
            sent[0][...] = total.astype(sent[0].dtype)


def against(left, at_ref, final_ref, came_ref, stored_ref, before, terms_ref, piece_ref, rows_ref):
    @pl.when(at_ref[0] != 0)
    def _():
        rows_ref[...] = final_ref[...]

    @pl.when(at_ref[0] == 0)
    def _():
        rows_ref[...] = came_ref[...]

    batches, slots, _ = stored_ref.shape
    wide = rows_ref.shape[1]
    term = lax.dot_general(
        rows_ref[...],
        stored_ref[:, :, left : left + wide].reshape(batches * slots, wide),
        (((1,), (1,)), ((), ())),
        preferred_element_type=jnp.float32,
    )
    terms_ref[...] = before[0][...] + term if before else term
    piece_ref[...] = rows_ref[pl.ds(pl.multiple_of(at_ref[1], 16), piece_ref.shape[0]), :]


def work_kernel(product, contract, joined, at_ref, after_ref, *refs):
    refs = list(refs)
    take = lambda n: [refs.pop(0) for _ in range(n)]
    if product:
        factors = take(2)
    if contract:
        rows = take(3)
        before = take(contract[1])
        pieces = take(joined)
    if product:
        (wide_ref,) = take(1)
        sent = take(1 if product[1] else 0)
    if contract:
        terms_ref, piece_ref = take(2)
    if joined:
        (whole_ref,) = take(1)
    if product:
        multiply(product[0], *factors, wide_ref, sent, *take(2))
    if contract:
        against(contract[0], at_ref, *rows, before, terms_ref, piece_ref, *take(1))
    if joined:
        left = 0
        for piece in pieces + [piece_ref]:
            whole_ref[:, left : left + piece.shape[1]] = piece[...]
            left += piece.shape[1]


def work(at, after, product=None, contract=None, pieces=()):
    operands, specs, shapes, scratch = [at, after], [SMEM, ANY], [], []
    product_at = contract_at = None
    if product:
        keys, weights, span, first = product
        depth, rows, wide = weights.shape[0], keys.shape[0], span[1] - span[0]
        product_at = (span[0], first)
        operands += [keys, weights]
        specs += [VMEM, ANY]
        shapes += [jax.ShapeDtypeStruct((rows, wide), jnp.float32)]
        shapes += [jax.ShapeDtypeStruct((rows, wide), jnp.bfloat16)] * first
        slots = STEPS if first else SLOTS
        scratch += [
            pltpu.VMEM((slots, depth // STEPS, wide), weights.dtype),
            pltpu.SemaphoreType.DMA((slots,)),
        ]
    if contract:
        final, came, stored, terms, left, block = contract
        rows, wide = final.shape
        before = [] if terms is None else [terms]
        contract_at = (left, len(before))
        operands += [final, came, stored, *before, *pieces]
        specs += [VMEM] * (3 + len(before) + len(pieces))
        shapes += [
            jax.ShapeDtypeStruct((rows, stored.shape[0] * stored.shape[1]), jnp.float32),
            jax.ShapeDtypeStruct((block, wide), jnp.bfloat16),
        ]
        scratch += [pltpu.VMEM((rows, wide), jnp.bfloat16)]
    if pieces:
        columns = sum(p.shape[1] for p in pieces) + wide
        shapes += [jax.ShapeDtypeStruct((block, columns), jnp.bfloat16)]
    return pl.pallas_call(
        functools.partial(work_kernel, product_at, contract_at, len(pieces)),
        in_specs=specs,
        out_specs=[VMEM] * len(shapes),
        out_shape=shapes,
        scratch_shapes=scratch,
        compiler_params=params(),
        cost_estimate=cost(),
        name="work",
    )(*operands)


def tick_kernel(names, outs, at_ref, after_ref, *refs):
    given = dict(zip(names, refs))
    made = dict(zip(outs, refs[len(names) :]))
    if "total" in made:
        total = given["wide"][...] + given["outer"][...].astype(jnp.float32)
        made["total"][...] = total
        made["across"][...] = total.astype(jnp.bfloat16)
    if "final" in made:
        final = (given["held"][...] + given["middle"][...].astype(jnp.float32)).astype(jnp.bfloat16)
        made["final"][...] = final
    if "along" in made:
        along = given["next"][...].astype(jnp.bfloat16)
        if "final" in made:
            along = jnp.where(at_ref[0] != 0, final, along)
        made["along"][...] = along


def tick(at, after, outs, **given):
    shape = next(iter(given.values())).shape
    wide = {"total": jnp.float32}
    made = pl.pallas_call(
        functools.partial(tick_kernel, tuple(given), outs),
        in_specs=[SMEM, ANY] + [VMEM] * len(given),
        out_specs=[VMEM] * len(outs),
        out_shape=[jax.ShapeDtypeStruct(shape, wide.get(name, jnp.bfloat16)) for name in outs],
        compiler_params=params(),
        cost_estimate=cost(),
        name="tick",
    )(at, after, *given.values())
    return dict(zip(outs, made))


def along_line(at, multiplied, contracted, count):
    wide, total, final = {}, {}, {}
    wide[0], sent = multiplied(0, at)
    outer = lax.ppermute(sent, "row", [(0, 1), (3, 2)])
    middle, after = None, sent
    if count > 1:
        (wide[1],) = multiplied(1, after)
        after = wide[1]
    for k in range(1, count + 2):
        outs, given = [], {}
        if k >= 2:
            outs += ["final"]
            given.update(held=total[k - 2], middle=middle)
        if 1 <= k <= count:
            outs += ["total", "across"]
            given.update(wide=wide[k - 1], outer=outer)
        if k < count:
            outs += ["along"]
            given.update(next=wide[k])
        made = tick(at, after, tuple(outs), **given)
        earlier = outer
        if k >= 2:
            final[k - 2] = made["final"]
        if 1 <= k <= count:
            total[k - 1] = made["total"]
            middle = lax.ppermute(made["across"], "row", [(1, 2), (2, 1)])
        pairs = ([(0, 1), (3, 2)] if k < count else []) + ([(1, 0), (2, 3)] if k >= 2 else [])
        sent = made["along"] if k < count else made["final"] if k >= 2 else made["across"]
        if pairs:
            outer = lax.ppermute(sent, "row", pairs)
        after = sent
        if k + 1 < count or k >= 3:
            product = k + 1 if k + 1 < count else None
            contract = (k - 3, final[k - 3], earlier) if k >= 3 else None
            out = multiplied(product, after, contract)
            if product is not None:
                wide[product] = out[0]
            after = out[-1]
    contracted(count - 1, final[count - 1], outer, after)


def select_kernel(row_ref, batch_ref, used_ref, length_ref, slot_ref, sums_ref, out_ref, held_ref):
    count, batches, rows, slots = held_ref.shape
    for i in range(count):
        for b in range(batches):
            held_ref[i, b] = sums_ref[i, :, b * slots : (b + 1) * slots]
    row = row_ref[0]
    column = lax.broadcasted_iota(jnp.int32, (rows, slots), 1)
    for place in range(out_ref.shape[1]):
        batch = batch_ref[row, place]
        slot = slot_ref[batch]
        owner = lax.div(slot, batches)
        length = jnp.where(place < used_ref[row], length_ref[batch], 0)
        value = held_ref[owner, slot - owner * batches]
        out_ref[0, place] = jnp.where(column < length, value, 0.0)


def selected(sums, row_index, pair_batch, pair_count, batch_length, batch_slot, batches):
    count, rows, wide = sums.shape
    slots = wide // batches
    places = pair_batch.shape[1]
    return pl.pallas_call(
        select_kernel,
        in_specs=[SMEM] * 5 + [VMEM],
        out_specs=VMEM,
        out_shape=jax.ShapeDtypeStruct((1, places, rows, slots), jnp.float32),
        scratch_shapes=[pltpu.VMEM((count, batches, rows, slots), jnp.float32)],
        cost_estimate=cost(),
        name="select",
    )(row_index[None], pair_batch, pair_count, batch_length, batch_slot, sums)


def shards(new_keys, precision, stored_keys, pair_batch, pair_count, batch_length, batch_slot):
    row_count = lax.axis_size("row")
    col_count = lax.axis_size("col")
    row_index = lax.axis_index("row")
    col_index = lax.axis_index("col")
    total_keys = new_keys.shape[0] * col_count
    block = total_keys // row_count
    batches = stored_keys.shape[0]
    half = row_count // 2

    away = jnp.where(row_index < half, half - 1 - row_index, row_index - half)
    at = jnp.stack([(away == 0).astype(jnp.int32), row_index * block])
    spans = ranges(precision.shape[1])
    count = len(spans)

    pieces, starts = gathered(new_keys, col_count, col_index)
    order = list(range(1, len(pieces))) + [0]
    keys = assembled([pieces[i] for i in order], jnp.stack([starts[i] for i in order]), total_keys)
    terms = None
    whitened = []

    def multiplied(part, after, contract=None):
        nonlocal terms
        product = None
        if part is not None:
            product = (keys, precision, spans[part], part == 0)
        if contract is not None:
            number, final, came = contract
            contract = (final, came, stored_keys, terms, spans[number][0], block)
        joined = whitened if contract is not None and number == count - 1 else []
        out = work(at, after, product, contract, joined)
        if contract is not None:
            terms = out[1 if product else 0]
            whitened.append(out[-1])
        return out

    def contracted(part, final, came, after):
        multiplied(None, after, (part, final, came))

    if row_count == 4:
        along_line(at, multiplied, contracted, count)
    else:
        after = at
        for part in range(count):
            wide = multiplied(part, after)[0]
            every = lax.psum(wide, "row").astype(jnp.bfloat16)
            contracted(part, every, every, wide)
            after = whitened[-1]

    share = block // col_count
    sums = terms.reshape(row_count, col_count, share, terms.shape[1])
    bit = 1
    while bit < col_count:
        if col_count == 8 and bit == 2:
            other = [lax.dynamic_index_in_dim(sums, (col_index // 2) ^ f, 1, keepdims=False) for f in range(4)]
            sums = other[0] + sum(flipped(other[f], 2 * f, col_count) for f in (3, 2, 1))
            sums = sums[:, None]
            break
        pairs = sums.reshape(row_count, sums.shape[1] // 2, 2, share, sums.shape[3])
        mine = (col_index // bit) % 2
        kept = lax.dynamic_index_in_dim(pairs, mine, 2, keepdims=False)
        left = lax.dynamic_index_in_dim(pairs, 1 - mine, 2, keepdims=False)
        sums = kept + flipped(left, bit, col_count)
        bit *= 2
    sums = lax.all_to_all(sums[:, 0], "row", split_axis=0, concat_axis=0, tiled=True)
    shares = selected(sums, row_index, pair_batch, pair_count, batch_length, batch_slot, batches)
    return (whitened[-1], shares)


def solution(mesh):
    placed = (P("col", "row"), P("row", "col"), P("row", None, "col"), P(), P(), P(), P())
    return jax.shard_map(
        shards,
        mesh=mesh,
        in_specs=placed,
        out_specs=(P("row", "col"), P("row", None, "col", None)),
        check_vma=False,
    )
```
